32 devices in a mesh: scan: 2 (over x), slab: 16 (over z, y, core).
Axes of the slice: x: 2, y: 2, z: 4, core: 2. Of those that a mesh axis runs over, the one named last changes fastest.
Arguments:
- image_coef: float32 [4, 12, 128, 384], P('scan', None, 'slab'), parts along dimension 0, may hold values from -6 to 6
- step_coef: float32 [4, 12, 128, 384], P('scan', None, 'slab'), parts along dimension 0, may hold values from -6 to 6
- coil_spec: float32 [96, 128, 384], P(('scan', 'slab')), parts along dimension 0, may hold values from -24 to 24
- step_spec: float32 [96, 128, 384], P(('scan', 'slab')), parts along dimension 0, may hold values from -12 to 12
- temporal_basis: float32 [30, 12], replicated, may hold values from -1 to 1
- sample_mask: int32 [256, 192], P('scan'), parts along dimension 0, may hold values from 0 to 1073741823, as said below
Outputs:
- grad_coef: float32 [4, 12, 128, 384], P('scan', None, 'slab'), parts along dimension 0
- grad_spec: float32 [96, 128, 384], P(('scan', 'slab')), parts along dimension 0
The draws below stay inside these ranges and needn't reach their ends.
There are 2 independent parts, one for each index of `scan`. The reference program is written for one: setup_inputs(seed, part) draws one part's arguments, and reference() takes and returns one part's arrays. A program takes and returns all parts, laid end to end along the dimension named above; an argument that names none is the same for every part. Nothing has to cross between parts.
Inputs may be any that keep to these rules, and one draw needn't show every extreme that they name: `sample_mask`: bit t of the entry for spectral point (kz, ky) is 1 where frame t samples that point, bits 30 and above are 0; the 7 x 7 points nearest the centre of k-space are sampled in every frame.
All inputs are finite; a program needn't handle non-finite values.
Results may differ from the reference program's by a relative error of at most 0.000071.
Values sent between devices are 32-bit elements; how exact they have to be, the bound alone decides.
A program may use at most 128 MiB of HBM per device.

```python
import math
import jax
import jax.numpy as jnp
from jax import lax

NY = 192
NZ = 128
COILS = 24
COEFS = 12
FRAMES = 30
XW = 2


def signed_freq_drawn(length):
    counter = jnp.arange(length, dtype=jnp.int32)
    return (counter + length // 2) % length - length // 2


def draw_sample_mask(key, part):
    freq_z = jnp.abs(signed_freq_drawn(NZ))
    freq_y = jnp.abs(signed_freq_drawn(NY))
    cycle_index = jnp.maximum(freq_z[:, None] * 8 // NZ, freq_y[None, :] * 8 // NY)
    thresholds = jnp.right_shift(jnp.full(cycle_index.shape, 32, dtype=jnp.int32), cycle_index)
    random_draws = jax.random.randint(jax.random.fold_in(key, 7), (FRAMES, NZ, NY), 0, 64, dtype=jnp.int32)
    frame_bits = (random_draws < thresholds[None]).astype(jnp.int32)
    central = (freq_z[:, None] < 4) & (freq_y[None, :] < 4)
    frame_bits = jnp.where(central[None], 1, frame_bits)
    powers = jnp.left_shift(jnp.ones((FRAMES,), dtype=jnp.int32), jnp.arange(FRAMES, dtype=jnp.int32))
    return jnp.sum(frame_bits * powers[:, None, None], axis=0).astype(jnp.int32)


def shard_levels(stream_key, dims, pieces, least, high):
    loudness, own = 1.0, jax.random.fold_in(stream_key, 6)
    for dim, blocks in pieces:
        steps = jnp.exp(jax.random.uniform(jax.random.fold_in(own, dim), (blocks,), jnp.float32, least / len(pieces), high / len(pieces)))
        loudness = loudness * jnp.repeat(steps, dims[dim] // blocks).reshape([-1 if axis == dim else 1 for axis in range(len(dims))])
    return loudness


def normal_values(own_key, shape, scale, most, cuts=(), held_as=jnp.bfloat16):
    loudness = shard_levels(own_key, shape, cuts, -0.22, 0.18) if cuts else 1.0
    drawn = jax.random.normal(own_key, shape, jnp.float32) * scale * loudness
    return jnp.minimum(jnp.maximum(drawn, -most), most).astype(held_as)


def setup_inputs(seed: int = 0, part: int = 0) -> dict:
    splits = jax.random.split(jax.random.key(seed), 7)
    part_splits = jax.random.split(jax.random.fold_in(splits[6], part), 7)
    return {
        "image_coef": normal_values(part_splits[0], (XW, COEFS, NZ, 2 * NY), 1.0, 6.0, ((2, 16),), jnp.float32),
        "step_coef": normal_values(part_splits[1], (XW, COEFS, NZ, 2 * NY), 1.0, 6.0, ((2, 16),), jnp.float32),
        "coil_spec": normal_values(part_splits[2], (XW * COILS, NZ, 2 * NY), 4.0, 24.0, ((0, 16),), jnp.float32),
        "step_spec": normal_values(part_splits[3], (XW * COILS, NZ, 2 * NY), 2.0, 12.0, ((0, 16),), jnp.float32),
        "temporal_basis": normal_values(splits[4], (FRAMES, COEFS), FRAMES ** -0.5, 1.0, (), jnp.float32),
        "sample_mask": draw_sample_mask(jax.random.fold_in(jax.random.fold_in(splits[6], part), 71), part),
    }


ALPHA = 0.5
SOBOLEV = 32.0

def signed_freq(length):
    counter = jnp.arange(length, dtype=jnp.int32)
    return (counter + length // 2) % length - length // 2

def dft_table(length, phase_sign):
    counter = jnp.arange(length, dtype=jnp.int32)
    phase_idx = counter[:, None] * counter[None, :] % length
    angles = phase_idx.astype(jnp.float32) * (2.0 * math.pi / length)
    norm_factor = 1.0 / math.sqrt(length)
    cosine = jnp.cos(angles) * norm_factor
    sine_part = jnp.sin(angles) * (norm_factor * phase_sign)
    return jnp.stack([jnp.stack([cosine, sine_part]), jnp.stack([-sine_part, cosine])])

def merged_table(phase_sign):
    dft_parts = dft_table(NY, phase_sign)
    return jnp.transpose(dft_parts, (0, 2, 1, 3)).reshape(2 * NY, 2 * NY)

def section_y(fields, merged):
    return jnp.dot(fields, merged, precision=lax.Precision.HIGHEST)

def section_z(fields, dft_parts):
    shaped = fields.reshape(fields.shape[:-1] + (2, NY))
    result = jnp.einsum('...zpy,pozw->...woy', shaped, dft_parts, precision=lax.Precision.HIGHEST)
    return result.reshape(fields.shape)

def sobolev_weights():
    freq_z = signed_freq(NZ).astype(jnp.float32) / NZ
    freq_y = signed_freq(NY).astype(jnp.float32) / NY
    radius = freq_z[:, None] ** 2 + freq_y[None, :] ** 2
    weight_plane = 1.0 / (1.0 + SOBOLEV * radius) ** 2
    return jnp.concatenate([weight_plane, weight_plane], axis=-1)

def sampled_frames(sample_mask):
    frames = jnp.arange(FRAMES, dtype=jnp.int32)
    shifted = jnp.right_shift(sample_mask[None], frames[:, None, None])
    return jnp.bitwise_and(shifted, 1).astype(jnp.float32)

def complex_products(first, second, third, fourth):
    first_re, first_im = (first[..., :NY], first[..., NY:])
    second_re, second_im = (second[..., :NY], second[..., NY:])
    third_re, third_im = (third[..., :NY], third[..., NY:])
    fourth_re, fourth_im = (fourth[..., :NY], fourth[..., NY:])
    real_part = first_re * second_re - first_im * second_im + third_re * fourth_re - third_im * fourth_im
    imag_part = first_re * second_im + first_im * second_re + third_re * fourth_im + third_im * fourth_re
    return jnp.concatenate([real_part, imag_part], axis=-1)

def conj_product(first, second):
    first_re, first_im = (first[..., :NY], first[..., NY:])
    second_re, second_im = (second[..., :NY], second[..., NY:])
    real_part = first_re * second_re + first_im * second_im
    imag_part = first_re * second_im - first_im * second_re
    return jnp.concatenate([real_part, imag_part], axis=-1)

def temporal_mix(spectra, temporal_basis, sampled):
    framed = jnp.einsum('tk,...kzv->...tzv', temporal_basis, spectra, precision=lax.Precision.HIGHEST)
    shaped = framed.reshape(framed.shape[:-1] + (2, NY)) * sampled[:, :, None, :]
    masked = shaped.reshape(framed.shape)
    return jnp.einsum('tk,...tzv->...kzv', temporal_basis, masked, precision=lax.Precision.HIGHEST)

def spectral_work(products, tables, temporal_basis, sampled):
    spectra = section_y(section_z(products, tables[2]), tables[0])
    mixed = temporal_mix(spectra, temporal_basis, sampled)
    return section_z(section_y(mixed, tables[1]), tables[3])

def reference(image_coef, step_coef, coil_spec, step_spec, temporal_basis, sample_mask):
    tables = (merged_table(-1.0), merged_table(1.0), dft_table(NZ, -1.0), dft_table(NZ, 1.0))
    weights = sobolev_weights()
    sampled = sampled_frames(sample_mask)
    coil_by_x = coil_spec.reshape(XW, COILS, NZ, 2 * NY)
    step_by_x = step_spec.reshape(XW, COILS, NZ, 2 * NY)

    def one_position(operands):
        coef_img, coef_step, coil_x, step_x = operands
        coil_img = section_z(section_y(coil_x * weights, tables[1]), tables[3])
        coil_dir = section_z(section_y(step_x * weights, tables[1]), tables[3])
        products = complex_products(coil_img[:, None], coef_step[None], coil_dir[:, None], coef_img[None])
        spread = spectral_work(products, tables, temporal_basis, sampled)
        coef_grad = lax.optimization_barrier(jnp.sum(conj_product(coil_img[:, None], spread), axis=0)) + ALPHA * coef_step
        coil_back = lax.optimization_barrier(jnp.sum(conj_product(coef_img[None], spread), axis=1))
        spec_grad = section_y(section_z(coil_back, tables[2]), tables[0]) * weights + ALPHA * step_x
        return (coef_grad, spec_grad)
    grad_coef, grad_spec = lax.map(one_position, (image_coef, step_coef, coil_by_x, step_by_x))
    return (grad_coef, grad_spec.reshape(XW * COILS, NZ, 2 * NY))
```

```python
import functools
import math

import jax
import jax.numpy as jnp
import ml_dtypes
import numpy as np
from jax import lax
from jax.experimental import pallas as pl
from jax.experimental.pallas import tpu as pltpu
from jax.sharding import PartitionSpec as P

NY = 192
NZ = 128
HY = NY // 2
COEFS = 12
FRAMES = 30
ALPHA = 0.5
SOBOLEV = 32.0
PAIRS = [(a, b) for a in range(COEFS) for b in range(a, COEFS)]
PAIR_AT = {p: i for i, p in enumerate(PAIRS)}
F32 = jnp.float32
BF16 = jnp.bfloat16


def complex_table(rows, cols, length, sign):
    idx = (np.asarray(rows)[:, None] * np.asarray(cols)[None, :]) % length
    angles = 2.0 * math.pi * idx / length
    scale = 1.0 / math.sqrt(length)
    return np.cos(angles) * scale, np.sin(angles) * (scale * sign)


def split_np(table):
    high = table.astype(np.float32).astype(ml_dtypes.bfloat16)
    low = (table - high.astype(np.float64)).astype(np.float32).astype(ml_dtypes.bfloat16)
    return high, low


def right_table(length, sign):
    c, s = complex_table(range(length), range(length), length, sign)
    high, low = split_np(np.block([[c, s], [-s, c]]))
    return np.concatenate([high, low, high], axis=0)


def left_table(rows, cols, length, sign):
    c, s = complex_table(rows, cols, length, sign)
    high, low = split_np(np.block([[c, -s], [s, c]]))
    return np.concatenate([high, high, low], axis=1)


EVEN = np.arange(0, NY, 2)
ODD = np.arange(1, NY, 2)
NEAR = np.arange(HY)


def make_tables():
    y_left = np.stack(
        [
            left_table(EVEN, NEAR, NY, -1.0),
            left_table(ODD, NEAR, NY, -1.0),
            left_table(NEAR, EVEN, NY, 1.0),
            left_table(NEAR, ODD, NY, 1.0),
        ]
    )
    y_right = np.stack([right_table(NY, -1.0), right_table(NY, 1.0)])
    z_right = np.stack([right_table(NZ, -1.0), right_table(NZ, 1.0)])
    fz = ((np.arange(NZ) + NZ // 2) % NZ - NZ // 2) / NZ
    fy = ((np.arange(NY) + NY // 2) % NY - NY // 2) / NY
    plane = 1.0 / (1.0 + SOBOLEV * (fz[:, None] ** 2 + fy[None, :] ** 2)) ** 2
    weights = np.concatenate([plane, plane], axis=1).astype(np.float32)
    return y_left, y_right, z_right, weights


def split(x):
    high = x.astype(BF16)
    low = (x - high.astype(F32)).astype(BF16)
    return high, low


def times_right(x, table):
    high, low = split(x)
    return jnp.dot(jnp.concatenate([high, high, low], axis=1), table, preferred_element_type=F32)


def times_left(table, x):
    high, low = split(x)
    return jnp.dot(table, jnp.concatenate([high, low, high], axis=0), preferred_element_type=F32)


def z_stage(re, im, table):
    out = times_right(jnp.concatenate([re, im], axis=1), table)
    return out[:, :NZ], out[:, NZ:]


def forward(planes, yl, zt):
    ups, downs = [], []
    for re, im in planes:
        ups.append(jnp.concatenate([re[:HY] + re[HY:], im[:HY] + im[HY:]], axis=0))
        downs.append(jnp.concatenate([re[:HY] - re[HY:], im[:HY] - im[HY:]], axis=0))
    even = times_left(yl[0], jnp.concatenate(ups, axis=1))
    odd = times_left(yl[1], jnp.concatenate(downs, axis=1))
    outs = []
    for i in range(2):
        at = slice(i * NZ, (i + 1) * NZ)
        re = jnp.concatenate([even[:HY, at], odd[:HY, at]], axis=0)
        im = jnp.concatenate([even[HY:, at], odd[HY:, at]], axis=0)
        outs.append(z_stage(re, im, zt[0]))
    return outs


def inverse(planes, yl, zt):
    evens, odds = [], []
    for re, im in planes:
        re, im = z_stage(re, im, zt[1])
        evens.append(jnp.concatenate([re[:HY], im[:HY]], axis=0))
        odds.append(jnp.concatenate([re[HY:], im[HY:]], axis=0))
    even = times_left(yl[2], jnp.concatenate(evens, axis=1))
    odd = times_left(yl[3], jnp.concatenate(odds, axis=1))
    near, far = even + odd, even - odd
    outs = []
    for i in range(2):
        at = slice(i * NZ, (i + 1) * NZ)
        re = jnp.concatenate([near[:HY, at], far[:HY, at]], axis=0)
        im = jnp.concatenate([near[HY:, at], far[HY:, at]], axis=0)
        outs.append((re, im))
    return outs


def coil_images(items, coil_ref, step_ref, weights, yr, zt, img):
    @pl.loop(0, items)
    def _(i):
        for which, ref in enumerate((coil_ref, step_ref)):
            rows = times_right(ref[i] * weights[...], yr[1])
            t = rows.T
            re, im = z_stage(t[:NY], t[NY:], zt[1])
            img[i, which, 0] = re
            img[i, which, 1] = im


def transposed_in(cols, colt, first, count):
    @pl.loop(first, first + count)
    def _(p):
        colt[p] = cols[p].T.reshape(2, NY, NZ)


def forward_pass(items, first_pair, pair_count, colt, img, spec, yl, zt):
    @pl.loop(first_pair * items, (first_pair + pair_count) * items)
    def _(step):
        pair, i = step // items, step % items
        planes = []
        for j in range(2):
            k = 2 * pair + j
            cr, ci = colt[2 * k, 0], colt[2 * k, 1]
            sr, si = colt[2 * k + 1, 0], colt[2 * k + 1, 1]
            ar, ai = img[i, 0, 0], img[i, 0, 1]
            dr, di = img[i, 1, 0], img[i, 1, 1]
            planes.append((ar * sr - ai * si + dr * cr - di * ci, ar * si + ai * sr + dr * ci + di * cr))
        for j, (re, im) in enumerate(forward(planes, yl, zt)):
            spec[i, 2 * pair + j, 0] = re
            spec[i, 2 * pair + j, 1] = im


def mix_pass(items, gram, spec):
    @pl.loop(0, NY // 8)
    def _(tile):
        rows = pl.ds(pl.multiple_of(tile * 8, 8), 8)
        for i in range(items):
            re = [spec[i, k, 0, rows, :] for k in range(COEFS)]
            im = [spec[i, k, 1, rows, :] for k in range(COEFS)]
            for k in range(COEFS):
                acc_re = acc_im = None
                for m in range(COEFS):
                    g = gram[PAIR_AT[(min(k, m), max(k, m))], rows, :]
                    acc_re = g * re[m] if acc_re is None else acc_re + g * re[m]
                    acc_im = g * im[m] if acc_im is None else acc_im + g * im[m]
                spec[i, k, 0, rows, :] = acc_re
                spec[i, k, 1, rows, :] = acc_im


def inverse_pass(items, first_pair, pair_count, colt, img, spec, grad, back, yl, zt):
    @pl.loop(first_pair * items, (first_pair + pair_count) * items)
    def _(step):
        pair, i = step // items, step % items
        outs = inverse([(spec[i, 2 * pair + j, 0], spec[i, 2 * pair + j, 1]) for j in range(2)], yl, zt)
        ar, ai = img[i, 0, 0], img[i, 0, 1]
        back_re, back_im = back[i, 0], back[i, 1]
        for j, (re, im) in enumerate(outs):
            k = 2 * pair + j
            cr, ci = colt[2 * k, 0], colt[2 * k, 1]
            back_re += cr * re + ci * im
            back_im += cr * im - ci * re
            grad_re = ar * re + ai * im
            grad_im = ar * im - ai * re

            @pl.when(i == 0)
            def _():
                grad[k, 0] = grad_re
                grad[k, 1] = grad_im

            @pl.when(i > 0)
            def _():
                grad[k, 0] += grad_re
                grad[k, 1] += grad_im

        back[i, 0] = back_re
        back[i, 1] = back_im


def coil_gradients(items, back, step_ref, weights, yr, zt, out):
    @pl.loop(0, items)
    def _(i):
        re, im = z_stage(back[i, 0], back[i, 1], zt[0])
        rows = jnp.concatenate([re, im], axis=0).T
        out[i] = times_right(rows, yr[0]) * weights[...] + ALPHA * step_ref[i]


def compute_kernel(items, cols, coil, step, gram, yl, yr, zt, weights, part, spec_out, colt, img, spec, grad, back):
    coil_images(items, coil, step, weights, yr, zt, img)
    transposed_in(cols, colt, 0, 2 * COEFS)
    back[...] = jnp.zeros_like(back)
    forward_pass(items, 0, COEFS // 2, colt, img, spec, yl, zt)
    mix_pass(items, gram, spec)
    inverse_pass(items, 0, COEFS // 2, colt, img, spec, grad, back, yl, zt)

    @pl.loop(0, COEFS)
    def _(k):
        part[k] = grad[k].reshape(2 * NY, NZ).T

    coil_gradients(items, back, step, weights, yr, zt, spec_out)


def compute(cols, coil, step, gram):
    items = coil.shape[0]
    tables = make_tables()
    vmem = pl.BlockSpec(memory_space=pltpu.VMEM)
    return pl.pallas_call(
        functools.partial(compute_kernel, items),
        out_shape=(
            jax.ShapeDtypeStruct((COEFS, NZ, 2 * NY), F32),
            jax.ShapeDtypeStruct(coil.shape, F32),
        ),
        in_specs=[vmem] * 8,
        out_specs=(vmem, vmem),
        scratch_shapes=[
            pltpu.VMEM((2 * COEFS, 2, NY, NZ), F32),
            pltpu.VMEM((items, 2, 2, NY, NZ), F32),
            pltpu.VMEM((items, COEFS, 2, NY, NZ), F32),
            pltpu.VMEM((COEFS, 2, NY, NZ), F32),
            pltpu.VMEM((items, 2, NY, NZ), F32),
        ],
        compiler_params=pltpu.CompilerParams(vmem_limit_bytes=56 * 2**20),
        cost_estimate=pl.CostEstimate(flops=16 * 10**9, bytes_accessed=20 * 2**20, transcendentals=0),
    )(cols, coil, step, gram, *[jnp.asarray(t) for t in tables])


def gram_planes(temporal_basis, sample_mask):
    first = np.array([p[0] for p in PAIRS])
    second = np.array([p[1] for p in PAIRS])
    outer = (temporal_basis[:, first] * temporal_basis[:, second]).T
    mask = sample_mask.T.reshape(HY, 2, NZ).transpose(1, 0, 2).reshape(NY, NZ)
    frames = jnp.arange(FRAMES, dtype=jnp.int32)
    bits = jnp.bitwise_and(jnp.right_shift(mask[None], frames[:, None, None]), 1).astype(F32)
    return jnp.einsum("qt,tyz->qyz", outer, bits, precision=lax.Precision.HIGHEST)


def gather_plain(both, devices):
    width_x = both.shape[0]
    groups = devices // width_x
    rep = jnp.broadcast_to(both[:, None], (width_x, groups) + both.shape[1:])
    rep = rep.reshape((devices * both.shape[1],) + both.shape[2:])
    return lax.all_to_all(rep, "slab", split_axis=0, concat_axis=1, tiled=True)


def scatter_plain(part, width_x, devices):
    homed = lax.all_to_all(part, "slab", split_axis=1, concat_axis=0, tiled=True)
    rows = part.shape[1] // devices
    return jnp.sum(homed.reshape(width_x, devices // width_x, COEFS, rows, 2 * NY), axis=1)


def shards(image_coef, step_coef, coil_spec, step_spec, temporal_basis, sample_mask):
    devices = lax.axis_size("slab")
    width_x, _, rows_z, _ = image_coef.shape
    both = jnp.stack([image_coef, step_coef], axis=2).reshape(width_x, 2 * COEFS, rows_z, 2 * NY)
    cols = gather_plain(both, devices)
    gram = gram_planes(temporal_basis, sample_mask)
    part, grad_spec = compute(cols, coil_spec, step_spec, gram)
    grad_coef = scatter_plain(part, width_x, devices) + ALPHA * step_coef
    return grad_coef, grad_spec


def solution(mesh):
    in_specs = (
        P("scan", None, "slab", None),
        P("scan", None, "slab", None),
        P(("scan", "slab"), None, None),
        P(("scan", "slab"), None, None),
        P(),
        P("scan", None),
    )
    out_specs = (P("scan", None, "slab", None), P(("scan", "slab"), None, None))
    return jax.shard_map(shards, mesh=mesh, in_specs=in_specs, out_specs=out_specs, check_vma=False)
```

```python
import functools
import math

import jax
import jax.numpy as jnp
import ml_dtypes
import numpy as np
from jax import lax
from jax.experimental import pallas as pl
from jax.experimental.pallas import tpu as pltpu
from jax.sharding import PartitionSpec as P

NY = 192
NZ = 128
HY = NY // 2
COEFS = 12
FRAMES = 30
ALPHA = 0.5
SOBOLEV = 32.0
PAIRS = [(a, b) for a in range(COEFS) for b in range(a, COEFS)]
PAIR_AT = {p: i for i, p in enumerate(PAIRS)}
F32 = jnp.float32
BF16 = jnp.bfloat16


def complex_table(rows, cols, length, sign):
    idx = (np.asarray(rows)[:, None] * np.asarray(cols)[None, :]) % length
    angles = 2.0 * math.pi * idx / length
    scale = 1.0 / math.sqrt(length)
    return np.cos(angles) * scale, np.sin(angles) * (scale * sign)


def split_np(table):
    high = table.astype(np.float32).astype(ml_dtypes.bfloat16)
    low = (table - high.astype(np.float64)).astype(np.float32).astype(ml_dtypes.bfloat16)
    return high, low


def right_table(length, sign):
    c, s = complex_table(range(length), range(length), length, sign)
    high, low = split_np(np.block([[c, s], [-s, c]]))
    return np.concatenate([high, low, high], axis=0)


def left_table(rows, cols, length, sign):
    c, s = complex_table(rows, cols, length, sign)
    high, low = split_np(np.block([[c, -s], [s, c]]))
    return np.concatenate([high, high, low], axis=1)


EVEN = np.arange(0, NY, 2)
ODD = np.arange(1, NY, 2)
NEAR = np.arange(HY)


def make_tables():
    y_left = np.stack(
        [
            left_table(EVEN, NEAR, NY, -1.0),
            left_table(ODD, NEAR, NY, -1.0),
            left_table(NEAR, EVEN, NY, 1.0),
            left_table(NEAR, ODD, NY, 1.0),
        ]
    )
    y_right = np.stack([right_table(NY, -1.0), right_table(NY, 1.0)])
    z_right = np.stack([right_table(NZ, -1.0), right_table(NZ, 1.0)])
    fz = ((np.arange(NZ) + NZ // 2) % NZ - NZ // 2) / NZ
    fy = ((np.arange(NY) + NY // 2) % NY - NY // 2) / NY
    plane = 1.0 / (1.0 + SOBOLEV * (fz[:, None] ** 2 + fy[None, :] ** 2)) ** 2
    weights = np.concatenate([plane, plane], axis=1).astype(np.float32)
    return y_left, y_right, z_right, weights


def split(x):
    high = x.astype(BF16)
    low = (x - high.astype(F32)).astype(BF16)
    return high, low


def times_right(x, table):
    high, low = split(x)
    return jnp.dot(jnp.concatenate([high, high, low], axis=1), table, preferred_element_type=F32)


def times_left(table, x):
    high, low = split(x)
    return jnp.dot(table, jnp.concatenate([high, low, high], axis=0), preferred_element_type=F32)


def z_stage(re, im, table):
    out = times_right(jnp.concatenate([re, im], axis=1), table)
    return out[:, :NZ], out[:, NZ:]


def forward(planes, yl, zt):
    ups, downs = [], []
    for re, im in planes:
        ups.append(jnp.concatenate([re[:HY] + re[HY:], im[:HY] + im[HY:]], axis=0))
        downs.append(jnp.concatenate([re[:HY] - re[HY:], im[:HY] - im[HY:]], axis=0))
    even = times_left(yl[0], jnp.concatenate(ups, axis=1))
    odd = times_left(yl[1], jnp.concatenate(downs, axis=1))
    outs = []
    for i in range(2):
        at = slice(i * NZ, (i + 1) * NZ)
        re = jnp.concatenate([even[:HY, at], odd[:HY, at]], axis=0)
        im = jnp.concatenate([even[HY:, at], odd[HY:, at]], axis=0)
        outs.append(z_stage(re, im, zt[0]))
    return outs


def inverse(planes, yl, zt):
    evens, odds = [], []
    for re, im in planes:
        re, im = z_stage(re, im, zt[1])
        evens.append(jnp.concatenate([re[:HY], im[:HY]], axis=0))
        odds.append(jnp.concatenate([re[HY:], im[HY:]], axis=0))
    even = times_left(yl[2], jnp.concatenate(evens, axis=1))
    odd = times_left(yl[3], jnp.concatenate(odds, axis=1))
    near, far = even + odd, even - odd
    outs = []
    for i in range(2):
        at = slice(i * NZ, (i + 1) * NZ)
        re = jnp.concatenate([near[:HY, at], far[:HY, at]], axis=0)
        im = jnp.concatenate([near[HY:, at], far[HY:, at]], axis=0)
        outs.append((re, im))
    return outs


def coil_images(items, coil_ref, step_ref, weights, yr, zt, img):
    @pl.loop(0, items)
    def _(i):
        for which, ref in enumerate((coil_ref, step_ref)):
            rows = times_right(ref[i] * weights[...], yr[1])
            t = rows.T
            re, im = z_stage(t[:NY], t[NY:], zt[1])
            img[i, which, 0] = re
            img[i, which, 1] = im


def transposed_in(cols, colt, first, count):
    @pl.loop(first, first + count)
    def _(p):
        colt[p] = cols[p].T.reshape(2, NY, NZ)


def forward_pass(items, first_pair, pair_count, colt, img, spec, yl, zt):
    @pl.loop(first_pair * items, (first_pair + pair_count) * items)
    def _(step):
        pair, i = step // items, step % items
        planes = []
        for j in range(2):
            k = 2 * pair + j
            cr, ci = colt[2 * k, 0], colt[2 * k, 1]
            sr, si = colt[2 * k + 1, 0], colt[2 * k + 1, 1]
            ar, ai = img[i, 0, 0], img[i, 0, 1]
            dr, di = img[i, 1, 0], img[i, 1, 1]
            planes.append((ar * sr - ai * si + dr * cr - di * ci, ar * si + ai * sr + dr * ci + di * cr))
        for j, (re, im) in enumerate(forward(planes, yl, zt)):
            spec[i, 2 * pair + j, 0] = re
            spec[i, 2 * pair + j, 1] = im


def mix_pass(items, gram, spec):
    @pl.loop(0, NY // 8)
    def _(tile):
        rows = pl.ds(pl.multiple_of(tile * 8, 8), 8)
        for i in range(items):
            re = [spec[i, k, 0, rows, :] for k in range(COEFS)]
            im = [spec[i, k, 1, rows, :] for k in range(COEFS)]
            for k in range(COEFS):
                acc_re = acc_im = None
                for m in range(COEFS):
                    g = gram[PAIR_AT[(min(k, m), max(k, m))], rows, :]
                    acc_re = g * re[m] if acc_re is None else acc_re + g * re[m]
                    acc_im = g * im[m] if acc_im is None else acc_im + g * im[m]
                spec[i, k, 0, rows, :] = acc_re
                spec[i, k, 1, rows, :] = acc_im


def inverse_pass(items, first_pair, pair_count, colt, img, spec, grad, back, yl, zt):
    @pl.loop(first_pair * items, (first_pair + pair_count) * items)
    def _(step):
        pair, i = step // items, step % items
        outs = inverse([(spec[i, 2 * pair + j, 0], spec[i, 2 * pair + j, 1]) for j in range(2)], yl, zt)
        ar, ai = img[i, 0, 0], img[i, 0, 1]
        back_re, back_im = back[i, 0], back[i, 1]
        for j, (re, im) in enumerate(outs):
            k = 2 * pair + j
            cr, ci = colt[2 * k, 0], colt[2 * k, 1]
            back_re += cr * re + ci * im
            back_im += cr * im - ci * re
            grad_re = ar * re + ai * im
            grad_im = ar * im - ai * re

            @pl.when(i == 0)
            def _():
                grad[k, 0] = grad_re
                grad[k, 1] = grad_im

            @pl.when(i > 0)
            def _():
                grad[k, 0] += grad_re
                grad[k, 1] += grad_im

        back[i, 0] = back_re
        back[i, 1] = back_im


def coil_gradients(items, back, step_ref, weights, yr, zt, out):
    @pl.loop(0, items)
    def _(i):
        re, im = z_stage(back[i, 0], back[i, 1], zt[0])
        rows = jnp.concatenate([re, im], axis=0).T
        out[i] = times_right(rows, yr[0]) * weights[...] + ALPHA * step_ref[i]


def compute_kernel(items, cols, coil, step, gram, yl, yr, zt, weights, part, spec_out, colt, img, spec, grad, back):
    coil_images(items, coil, step, weights, yr, zt, img)
    transposed_in(cols, colt, 0, 2 * COEFS)
    back[...] = jnp.zeros_like(back)
    forward_pass(items, 0, COEFS // 2, colt, img, spec, yl, zt)
    mix_pass(items, gram, spec)
    inverse_pass(items, 0, COEFS // 2, colt, img, spec, grad, back, yl, zt)

    @pl.loop(0, COEFS)
    def _(k):
        part[k] = grad[k].reshape(2 * NY, NZ).T

    coil_gradients(items, back, step, weights, yr, zt, spec_out)


def compute(cols, coil, step, gram):
    items = coil.shape[0]
    tables = make_tables()
    vmem = pl.BlockSpec(memory_space=pltpu.VMEM)
    return pl.pallas_call(
        functools.partial(compute_kernel, items),
        out_shape=(
            jax.ShapeDtypeStruct((COEFS, NZ, 2 * NY), F32),
            jax.ShapeDtypeStruct(coil.shape, F32),
        ),
        in_specs=[vmem] * 8,
        out_specs=(vmem, vmem),
        scratch_shapes=[
            pltpu.VMEM((2 * COEFS, 2, NY, NZ), F32),
            pltpu.VMEM((items, 2, 2, NY, NZ), F32),
            pltpu.VMEM((items, COEFS, 2, NY, NZ), F32),
            pltpu.VMEM((COEFS, 2, NY, NZ), F32),
            pltpu.VMEM((items, 2, NY, NZ), F32),
        ],
        compiler_params=pltpu.CompilerParams(vmem_limit_bytes=56 * 2**20),
        cost_estimate=pl.CostEstimate(flops=16 * 10**9, bytes_accessed=20 * 2**20, transcendentals=0),
    )(cols, coil, step, gram, *[jnp.asarray(t) for t in tables])


def gram_planes(temporal_basis, sample_mask):
    first = np.array([p[0] for p in PAIRS])
    second = np.array([p[1] for p in PAIRS])
    outer = (temporal_basis[:, first] * temporal_basis[:, second]).T
    mask = sample_mask.T.reshape(HY, 2, NZ).transpose(1, 0, 2).reshape(NY, NZ)
    frames = jnp.arange(FRAMES, dtype=jnp.int32)
    bits = jnp.bitwise_and(jnp.right_shift(mask[None], frames[:, None, None]), 1).astype(F32)
    return jnp.einsum("qt,tyz->qyz", outer, bits, precision=lax.Precision.HIGHEST)


def gather_plain(both, devices):
    width_x = both.shape[0]
    groups = devices // width_x
    rep = jnp.broadcast_to(both[:, None], (width_x, groups) + both.shape[1:])
    rep = rep.reshape((devices * both.shape[1],) + both.shape[2:])
    return lax.all_to_all(rep, "slab", split_axis=0, concat_axis=1, tiled=True)


def scatter_plain(part, width_x, devices):
    homed = lax.all_to_all(part, "slab", split_axis=1, concat_axis=0, tiled=True)
    rows = part.shape[1] // devices
    return jnp.sum(homed.reshape(width_x, devices // width_x, COEFS, rows, 2 * NY), axis=1)


MESH = pl.DeviceIdType.MESH


class Place:
    def __init__(self):
        me = lax.axis_index("slab")
        self.z, self.y, self.c = me // 4, (me // 2) % 2, me % 2
        self.half = self.z // 2
        self.pair = 4 * self.half + 1 - self.z
        self.near = 2 - self.half
        self.far = 3 - 3 * self.half
        self.gate = self.z == 1 + self.half

    def slab(self, z=None, y=None, c=None):
        z = self.z if z is None else z
        y = self.y if y is None else y
        c = self.c if c is None else c
        return z * 4 + y * 2 + c


def rcopy(src, dst, send, recv, slab):
    return pltpu.make_async_remote_copy(
        src_ref=src, dst_ref=dst, send_sem=send, recv_sem=recv, device_id={"slab": slab}, device_id_type=MESH
    )


def greet(at):
    barrier = pltpu.get_barrier_semaphore()

    def hello(slab):
        pl.semaphore_signal(barrier, inc=1, device_id={"slab": slab}, device_id_type=MESH)

    hello(at.slab(z=at.pair))
    hello(at.slab(y=1 - at.y))
    hello(at.slab(c=1 - at.c))
    hello(at.slab(z=at.near))

    @pl.when(at.gate)
    def _():
        hello(at.slab(z=at.far))
        pl.semaphore_wait(barrier, 5)

    @pl.when(jnp.logical_not(at.gate))
    def _():
        pl.semaphore_wait(barrier, 4)


class Gather:
    def __init__(self, at, both, cols, sems, chunks):
        self.at, self.both, self.cols, self.chunks = at, both, cols, chunks
        self.own_sem, self.zs, self.zr, self.fs, self.ys, self.yr, self.cs, self.cr = sems
        self.size = 2 * COEFS // chunks

    def block(self, ch, z, y=None, c=None):
        at = self.at
        return self.cols.at[
            pl.ds(ch * self.size, self.size), z, at.y if y is None else y, at.c if c is None else c
        ]

    def mine(self, ch, x):
        return self.both.at[x, pl.ds(ch * self.size, self.size)]

    def own(self, ch):
        return pltpu.make_async_copy(self.mine(ch, self.at.half), self.block(ch, self.at.z), self.own_sem.at[ch])

    def to_pair(self, ch):
        at = self.at
        return rcopy(
            self.mine(ch, at.half), self.block(ch, at.z), self.zs.at[ch, 0], self.zr.at[ch, at.z], at.slab(z=at.pair)
        )

    def to_gate(self, ch):
        at = self.at
        return rcopy(
            self.mine(ch, 1 - at.half), self.block(ch, at.z), self.zs.at[ch, 1], self.zr.at[ch, at.z], at.slab(z=at.near)
        )

    def onward(self, ch, z, i):
        at = self.at
        return rcopy(self.block(ch, z), self.block(ch, z), self.fs.at[ch, i], self.zr.at[ch, z], at.slab(z=at.pair))

    def z_arrival(self, ch, z):
        return rcopy(self.block(ch, z), self.block(ch, z), self.fs.at[ch, 0], self.zr.at[ch, z], self.at.slab(z=self.at.pair))

    def across(self, ch, z, src=None):
        at = self.at
        src = self.block(ch, z) if src is None else src
        return rcopy(src, self.block(ch, z), self.ys.at[ch, z], self.yr.at[ch, z], at.slab(y=1 - at.y))

    def y_arrival(self, ch, z):
        at = self.at
        dst = self.block(ch, z, y=1 - at.y)
        return rcopy(dst, dst, self.ys.at[ch, z], self.yr.at[ch, z], at.slab(y=1 - at.y))

    def core(self, ch, c=None):
        at = self.at
        dst = self.cols.at[pl.ds(ch * self.size, self.size), :, :, at.c if c is None else c]
        return rcopy(dst, dst, self.cs.at[ch], self.cr.at[ch], at.slab(c=1 - at.c))

    def start(self, ch):
        self.own(ch).start()
        self.to_gate(ch).start()
        self.to_pair(ch).start()
        self.across(ch, self.at.z, self.mine(ch, self.at.half)).start()

    def on_z(self, ch):
        at = self.at
        self.z_arrival(ch, at.pair).wait_recv()
        self.across(ch, at.pair).start()
        for i, z in enumerate((at.near, at.far)):
            self.z_arrival(ch, z).wait_recv()

            @pl.when(at.gate)
            def _():
                self.onward(ch, z, i).start()

            self.across(ch, z).start()

    def on_y(self, ch):
        self.own(ch).wait()
        for z in range(4):
            self.y_arrival(ch, z).wait_recv()
        self.core(ch).start()

    def on_core(self, ch):
        self.core(ch, 1 - self.at.c).wait_recv()

    def finish(self, ch):
        at = self.at
        self.to_gate(ch).wait_send()
        self.to_pair(ch).wait_send()
        self.across(ch, at.z, self.mine(ch, at.half)).wait_send()
        for z in (at.pair, at.near, at.far):
            self.across(ch, z).wait_send()

        @pl.when(at.gate)
        def _():
            for i, z in enumerate((at.near, at.far)):
                self.onward(ch, z, i).wait_send()

        self.core(ch).wait_send()


def gather_sems(chunks):
    dma = pltpu.SemaphoreType.DMA
    return [
        dma((chunks,)),
        dma((chunks, 2)),
        dma((chunks, 4)),
        dma((chunks, 2)),
        dma((chunks, 4)),
        dma((chunks, 4)),
        dma((chunks,)),
        dma((chunks,)),
    ]


class Scatter:
    def __init__(self, at, part, step, out, bufs, sems, chunks):
        self.at, self.part, self.step, self.out = at, part, step, out
        self.from_core, self.from_y, self.from_z, self.from_far = bufs
        self.cs, self.cr, self.ys, self.yr, self.zs, self.zr, self.fs, self.fr = sems
        self.size = COEFS // chunks

    def ks(self, ch):
        return pl.ds(ch * self.size, self.size)

    def core(self, ch):
        at = self.at
        return rcopy(
            self.part.at[self.ks(ch), :, :, 1 - at.c],
            self.from_core.at[self.ks(ch)],
            self.cs.at[ch],
            self.cr.at[ch],
            at.slab(c=1 - at.c),
        )

    def across(self, ch):
        at = self.at
        return rcopy(
            self.from_core.at[self.ks(ch), :, 1 - at.y],
            self.from_y.at[self.ks(ch)],
            self.ys.at[ch],
            self.yr.at[ch],
            at.slab(y=1 - at.y),
        )

    def inward(self, ch):
        at = self.at
        rows = pl.ds(1 - at.half, 3)
        return rcopy(
            self.from_y.at[self.ks(ch), rows],
            self.from_z.at[self.ks(ch), rows],
            self.zs.at[ch],
            self.zr.at[ch],
            at.slab(z=at.pair),
        )

    def outward(self, ch, z):
        at = self.at
        return rcopy(
            self.from_y.at[self.ks(ch), z],
            self.from_z.at[self.ks(ch), z],
            self.zs.at[ch],
            self.zr.at[ch],
            at.slab(z=at.pair),
        )

    def home(self, ch, z, i):
        at = self.at
        return rcopy(
            self.from_z.at[self.ks(ch), z], self.from_far.at[self.ks(ch)], self.fs.at[ch, i], self.fr.at[ch], at.slab(z=z)
        )

    def start(self, ch):
        self.core(ch).start()

    def on_core(self, ch):
        at, ks = self.at, self.ks(ch)
        self.core(ch).wait_recv()
        self.from_core[ks] += self.part[ks, :, :, at.c]
        self.across(ch).start()

    def on_y(self, ch):
        at, ks = self.at, self.ks(ch)
        self.across(ch).wait_recv()
        self.from_y[ks] += self.from_core[ks, :, at.y]

        @pl.when(at.gate)
        def _():
            self.outward(ch, at.pair).start()

        @pl.when(jnp.logical_not(at.gate))
        def _():
            self.inward(ch).start()

    def on_z(self, ch):
        at, ks = self.at, self.ks(ch)

        @pl.when(at.gate)
        def _():
            self.inward(ch).wait_recv()
            for i, z in enumerate((at.near, at.far)):
                self.from_z[ks, z] += self.from_y[ks, z]
                self.home(ch, z, i).start()

        @pl.when(jnp.logical_not(at.gate))
        def _():
            self.outward(ch, at.z).wait_recv()

        self.out[at.half, ks] = self.from_y[ks, at.z] + self.from_z[ks, at.z] + ALPHA * self.step[at.half, ks]

    def on_far(self, ch):
        at, ks = self.at, self.ks(ch)
        self.home(ch, at.near, 0).wait_recv()
        self.out[1 - at.half, ks] = self.from_far[ks] + ALPHA * self.step[1 - at.half, ks]

    def finish(self, ch):
        at = self.at
        self.core(ch).wait_send()
        self.across(ch).wait_send()

        @pl.when(at.gate)
        def _():
            self.outward(ch, at.pair).wait_send()
            for i, z in enumerate((at.near, at.far)):
                self.home(ch, z, i).wait_send()

        @pl.when(jnp.logical_not(at.gate))
        def _():
            self.inward(ch).wait_send()


def scatter_scratch():
    return [
        pltpu.VMEM((COEFS, 4, 2, 8, 2 * NY), F32),
        pltpu.VMEM((COEFS, 4, 8, 2 * NY), F32),
        pltpu.VMEM((COEFS, 4, 8, 2 * NY), F32),
        pltpu.VMEM((COEFS, 8, 2 * NY), F32),
    ]


def scatter_sems(chunks):
    dma = pltpu.SemaphoreType.DMA
    return [dma((chunks,))] * 6 + [dma((chunks, 2)), dma((chunks,))]


def each(chunks, step):
    @pl.loop(0, chunks)
    def _(ch):
        step(ch)


def gather_kernel(chunks, both, cols, *sems):
    at = Place()
    greet(at)
    g = Gather(at, both, cols, sems, chunks)
    for step in (g.start, g.on_z, g.on_y, g.on_core, g.finish):
        each(chunks, step)


def gather_near(both):
    chunks = 3
    vmem = pl.BlockSpec(memory_space=pltpu.VMEM)
    return pl.pallas_call(
        functools.partial(gather_kernel, chunks),
        out_shape=jax.ShapeDtypeStruct((2 * COEFS, 4, 2, 2, 8, 2 * NY), F32),
        in_specs=[vmem],
        out_specs=vmem,
        scratch_shapes=gather_sems(chunks),
        compiler_params=pltpu.CompilerParams(collective_id=0, has_side_effects=True, vmem_limit_bytes=32 * 2**20),
    )(both)


def scatter_kernel(chunks, part, step, out, *scratch):
    at = Place()
    greet(at)
    s = Scatter(at, part, step, out, scratch[:4], scratch[4:], chunks)
    for stage in (s.start, s.on_core, s.on_y, s.on_z, s.on_far, s.finish):
        each(chunks, stage)


def scatter_near(part, step):
    chunks = 3
    vmem = pl.BlockSpec(memory_space=pltpu.VMEM)
    return pl.pallas_call(
        functools.partial(scatter_kernel, chunks),
        out_shape=jax.ShapeDtypeStruct(step.shape, F32),
        in_specs=[vmem] * 2,
        out_specs=vmem,
        scratch_shapes=scatter_scratch() + scatter_sems(chunks),
        compiler_params=pltpu.CompilerParams(collective_id=1, has_side_effects=True, vmem_limit_bytes=32 * 2**20),
    )(part, step)


def shards(image_coef, step_coef, coil_spec, step_spec, temporal_basis, sample_mask):
    devices = lax.axis_size("slab")
    width_x, _, rows_z, _ = image_coef.shape
    both = jnp.stack([image_coef, step_coef], axis=2).reshape(width_x, 2 * COEFS, rows_z, 2 * NY)
    gram = gram_planes(temporal_basis, sample_mask)
    if devices == 16 and width_x == 2 and rows_z == 8:
        cols = gather_near(both).reshape(2 * COEFS, NZ, 2 * NY)
        part, grad_spec = compute(cols, coil_spec, step_spec, gram)
        grad_coef = scatter_near(part.reshape(COEFS, 4, 2, 2, rows_z, 2 * NY), step_coef)
    else:
        cols = gather_plain(both, devices)
        part, grad_spec = compute(cols, coil_spec, step_spec, gram)
        grad_coef = scatter_plain(part, width_x, devices) + ALPHA * step_coef
    return grad_coef, grad_spec


def solution(mesh):
    in_specs = (
        P("scan", None, "slab", None),
        P("scan", None, "slab", None),
        P(("scan", "slab"), None, None),
        P(("scan", "slab"), None, None),
        P(),
        P("scan", None),
    )
    out_specs = (P("scan", None, "slab", None), P(("scan", "slab"), None, None))
    return jax.shard_map(shards, mesh=mesh, in_specs=in_specs, out_specs=out_specs, check_vma=False)
```

```python
import functools
import math

import jax
import jax.numpy as jnp
import ml_dtypes
import numpy as np
from jax import lax
from jax.experimental import pallas as pl
from jax.experimental.pallas import tpu as pltpu
from jax.sharding import PartitionSpec as P

NY = 192
NZ = 128
HY = NY // 2
COEFS = 12
FRAMES = 30
ALPHA = 0.5
SOBOLEV = 32.0
PAIRS = [(a, b) for a in range(COEFS) for b in range(a, COEFS)]
PAIR_AT = {p: i for i, p in enumerate(PAIRS)}
F32 = jnp.float32
BF16 = jnp.bfloat16


def complex_table(rows, cols, length, sign):
    idx = (np.asarray(rows)[:, None] * np.asarray(cols)[None, :]) % length
    angles = 2.0 * math.pi * idx / length
    scale = 1.0 / math.sqrt(length)
    return np.cos(angles) * scale, np.sin(angles) * (scale * sign)


def split_np(table):
    high = table.astype(np.float32).astype(ml_dtypes.bfloat16)
    low = (table - high.astype(np.float64)).astype(np.float32).astype(ml_dtypes.bfloat16)
    return high, low


def right_table(length, sign):
    c, s = complex_table(range(length), range(length), length, sign)
    high, low = split_np(np.block([[c, s], [-s, c]]))
    return np.concatenate([high, low, high], axis=0)


def left_table(rows, cols, length, sign):
    c, s = complex_table(rows, cols, length, sign)
    high, low = split_np(np.block([[c, -s], [s, c]]))
    return np.concatenate([high, high, low], axis=1)


EVEN = np.arange(0, NY, 2)
ODD = np.arange(1, NY, 2)
NEAR = np.arange(HY)


def make_tables():
    y_left = np.stack(
        [
            left_table(EVEN, NEAR, NY, -1.0),
            left_table(ODD, NEAR, NY, -1.0),
            left_table(NEAR, EVEN, NY, 1.0),
            left_table(NEAR, ODD, NY, 1.0),
        ]
    )
    y_right = np.stack([right_table(NY, -1.0), right_table(NY, 1.0)])
    z_right = np.stack([right_table(NZ, -1.0), right_table(NZ, 1.0)])
    fz = ((np.arange(NZ) + NZ // 2) % NZ - NZ // 2) / NZ
    fy = ((np.arange(NY) + NY // 2) % NY - NY // 2) / NY
    plane = 1.0 / (1.0 + SOBOLEV * (fz[:, None] ** 2 + fy[None, :] ** 2)) ** 2
    weights = np.concatenate([plane, plane], axis=1).astype(np.float32)
    return y_left, y_right, z_right, weights


def split(x):
    high = x.astype(BF16)
    low = (x - high.astype(F32)).astype(BF16)
    return high, low


def times_right(x, table):
    high, low = split(x)
    return jnp.dot(jnp.concatenate([high, high, low], axis=1), table, preferred_element_type=F32)


def times_left(table, x):
    high, low = split(x)
    return jnp.dot(table, jnp.concatenate([high, low, high], axis=0), preferred_element_type=F32)


def z_stage(re, im, table):
    out = times_right(jnp.concatenate([re, im], axis=1), table)
    return out[:, :NZ], out[:, NZ:]


def forward(planes, yl, zt):
    ups, downs = [], []
    for re, im in planes:
        ups.append(jnp.concatenate([re[:HY] + re[HY:], im[:HY] + im[HY:]], axis=0))
        downs.append(jnp.concatenate([re[:HY] - re[HY:], im[:HY] - im[HY:]], axis=0))
    even = times_left(yl[0], jnp.concatenate(ups, axis=1))
    odd = times_left(yl[1], jnp.concatenate(downs, axis=1))
    outs = []
    for i in range(2):
        at = slice(i * NZ, (i + 1) * NZ)
        re = jnp.concatenate([even[:HY, at], odd[:HY, at]], axis=0)
        im = jnp.concatenate([even[HY:, at], odd[HY:, at]], axis=0)
        outs.append(z_stage(re, im, zt[0]))
    return outs


def inverse(planes, yl, zt):
    evens, odds = [], []
    for re, im in planes:
        re, im = z_stage(re, im, zt[1])
        evens.append(jnp.concatenate([re[:HY], im[:HY]], axis=0))
        odds.append(jnp.concatenate([re[HY:], im[HY:]], axis=0))
    even = times_left(yl[2], jnp.concatenate(evens, axis=1))
    odd = times_left(yl[3], jnp.concatenate(odds, axis=1))
    near, far = even + odd, even - odd
    outs = []
    for i in range(2):
        at = slice(i * NZ, (i + 1) * NZ)
        re = jnp.concatenate([near[:HY, at], far[:HY, at]], axis=0)
        im = jnp.concatenate([near[HY:, at], far[HY:, at]], axis=0)
        outs.append((re, im))
    return outs


def coil_images(items, coil_ref, step_ref, weights, yr, zt, img):
    @pl.loop(0, items)
    def _(i):
        for which, ref in enumerate((coil_ref, step_ref)):
            rows = times_right(ref[i] * weights[...], yr[1])
            t = rows.T
            re, im = z_stage(t[:NY], t[NY:], zt[1])
            img[i, which, 0] = re
            img[i, which, 1] = im


def transposed_in(cols, colt, first, count):
    @pl.loop(first, first + count)
    def _(p):
        colt[p] = cols[p].reshape(NZ, 2 * NY).T.reshape(2, NY, NZ)


def forward_pass(items, first_pair, pair_count, colt, img, spec, yl, zt):
    @pl.loop(first_pair * items, (first_pair + pair_count) * items)
    def _(step):
        pair, i = step // items, step % items
        planes = []
        for j in range(2):
            k = 2 * pair + j
            cr, ci = colt[2 * k, 0], colt[2 * k, 1]
            sr, si = colt[2 * k + 1, 0], colt[2 * k + 1, 1]
            ar, ai = img[i, 0, 0], img[i, 0, 1]
            dr, di = img[i, 1, 0], img[i, 1, 1]
            planes.append((ar * sr - ai * si + dr * cr - di * ci, ar * si + ai * sr + dr * ci + di * cr))
        for j, (re, im) in enumerate(forward(planes, yl, zt)):
            spec[i, 2 * pair + j, 0] = re
            spec[i, 2 * pair + j, 1] = im


def mix_pass(items, gram, spec):
    @pl.loop(0, NY // 8)
    def _(tile):
        rows = pl.ds(pl.multiple_of(tile * 8, 8), 8)
        for i in range(items):
            re = [spec[i, k, 0, rows, :] for k in range(COEFS)]
            im = [spec[i, k, 1, rows, :] for k in range(COEFS)]
            for k in range(COEFS):
                acc_re = acc_im = None
                for m in range(COEFS):
                    first = PAIR_AT[(min(k, m), max(k, m))] * NY + tile * 8
                    g = gram[pl.ds(pl.multiple_of(first, 8), 8), :]
                    acc_re = g * re[m] if acc_re is None else acc_re + g * re[m]
                    acc_im = g * im[m] if acc_im is None else acc_im + g * im[m]
                spec[i, k, 0, rows, :] = acc_re
                spec[i, k, 1, rows, :] = acc_im


def inverse_pass(items, first_pair, pair_count, colt, img, spec, grad, back, yl, zt):
    @pl.loop(first_pair * items, (first_pair + pair_count) * items)
    def _(step):
        pair, i = step // items, step % items
        outs = inverse([(spec[i, 2 * pair + j, 0], spec[i, 2 * pair + j, 1]) for j in range(2)], yl, zt)
        ar, ai = img[i, 0, 0], img[i, 0, 1]
        back_re, back_im = back[i, 0], back[i, 1]
        for j, (re, im) in enumerate(outs):
            k = 2 * pair + j
            cr, ci = colt[2 * k, 0], colt[2 * k, 1]
            back_re += cr * re + ci * im
            back_im += cr * im - ci * re
            grad_re = ar * re + ai * im
            grad_im = ar * im - ai * re

            @pl.when(i == 0)
            def _():
                grad[k, 0] = grad_re
                grad[k, 1] = grad_im

            @pl.when(i > 0)
            def _():
                grad[k, 0] += grad_re
                grad[k, 1] += grad_im

        back[i, 0] = back_re
        back[i, 1] = back_im


def coil_gradients(first, count, back, step_ref, weights, yr, zt, out):
    @pl.loop(first, first + count)
    def _(i):
        re, im = z_stage(back[i, 0], back[i, 1], zt[0])
        rows = jnp.concatenate([re, im], axis=0).T
        out[i] = times_right(rows, yr[0]) * weights[...] + ALPHA * step_ref[i]


def compute_kernel(items, cols, coil, step, gram, yl, yr, zt, weights, part, spec_out, colt, img, spec, grad, back):
    coil_images(items, coil, step, weights, yr, zt, img)
    transposed_in(cols, colt, 0, 2 * COEFS)
    back[...] = jnp.zeros_like(back)
    forward_pass(items, 0, COEFS // 2, colt, img, spec, yl, zt)
    mix_pass(items, gram, spec)
    inverse_pass(items, 0, COEFS // 2, colt, img, spec, grad, back, yl, zt)

    @pl.loop(0, COEFS)
    def _(k):
        part[k] = grad[k].reshape(2 * NY, NZ).T

    coil_gradients(0, items, back, step, weights, yr, zt, spec_out)


def compute(cols, coil, step, gram):
    items = coil.shape[0]
    tables = make_tables()
    vmem = pl.BlockSpec(memory_space=pltpu.VMEM)
    return pl.pallas_call(
        functools.partial(compute_kernel, items),
        out_shape=(
            jax.ShapeDtypeStruct((COEFS, NZ, 2 * NY), F32),
            jax.ShapeDtypeStruct(coil.shape, F32),
        ),
        in_specs=[vmem] * 8,
        out_specs=(vmem, vmem),
        scratch_shapes=[
            pltpu.VMEM((2 * COEFS, 2, NY, NZ), F32),
            pltpu.VMEM((items, 2, 2, NY, NZ), F32),
            pltpu.VMEM((items, COEFS, 2, NY, NZ), F32),
            pltpu.VMEM((COEFS, 2, NY, NZ), F32),
            pltpu.VMEM((items, 2, NY, NZ), F32),
        ],
        compiler_params=pltpu.CompilerParams(vmem_limit_bytes=56 * 2**20),
        cost_estimate=pl.CostEstimate(flops=16 * 10**9, bytes_accessed=20 * 2**20, transcendentals=0),
    )(cols, coil, step, gram, *[jnp.asarray(t) for t in tables])


def gram_planes(temporal_basis, sample_mask):
    first = np.array([p[0] for p in PAIRS])
    second = np.array([p[1] for p in PAIRS])
    outer = (temporal_basis[:, first] * temporal_basis[:, second]).T
    mask = sample_mask.T.reshape(HY, 2, NZ).transpose(1, 0, 2).reshape(NY, NZ)
    frames = jnp.arange(FRAMES, dtype=jnp.int32)
    bits = jnp.bitwise_and(jnp.right_shift(mask[None], frames[:, None, None]), 1).astype(F32)
    return jnp.einsum("qt,tyz->qyz", outer, bits, precision=lax.Precision.HIGHEST)


def gather_plain(both, devices):
    width_x = both.shape[0]
    groups = devices // width_x
    rep = jnp.broadcast_to(both[:, None], (width_x, groups) + both.shape[1:])
    rep = rep.reshape((devices * both.shape[1],) + both.shape[2:])
    return lax.all_to_all(rep, "slab", split_axis=0, concat_axis=1, tiled=True)


def scatter_plain(part, width_x, devices):
    homed = lax.all_to_all(part, "slab", split_axis=1, concat_axis=0, tiled=True)
    rows = part.shape[1] // devices
    return jnp.sum(homed.reshape(width_x, devices // width_x, COEFS, rows, 2 * NY), axis=1)


MESH = pl.DeviceIdType.MESH


class Place:
    def __init__(self):
        me = lax.axis_index("slab")
        self.z, self.y, self.c = me // 4, (me // 2) % 2, me % 2
        self.half = self.z // 2
        self.pair = 4 * self.half + 1 - self.z
        self.near = 2 - self.half
        self.far = 3 - 3 * self.half
        self.gate = self.z == 1 + self.half

    def slab(self, z=None, y=None, c=None):
        z = self.z if z is None else z
        y = self.y if y is None else y
        c = self.c if c is None else c
        return z * 4 + y * 2 + c


def rcopy(src, dst, send, recv, slab):
    return pltpu.make_async_remote_copy(
        src_ref=src, dst_ref=dst, send_sem=send, recv_sem=recv, device_id={"slab": slab}, device_id_type=MESH
    )


def greet(at):
    barrier = pltpu.get_barrier_semaphore()

    def hello(slab):
        pl.semaphore_signal(barrier, inc=1, device_id={"slab": slab}, device_id_type=MESH)

    hello(at.slab(z=at.pair))
    hello(at.slab(y=1 - at.y))
    hello(at.slab(c=1 - at.c))
    hello(at.slab(z=at.near))

    @pl.when(at.gate)
    def _():
        hello(at.slab(z=at.far))
        pl.semaphore_wait(barrier, 5)

    @pl.when(jnp.logical_not(at.gate))
    def _():
        pl.semaphore_wait(barrier, 4)


class Gather:
    def __init__(self, at, both, cols, sems, chunks):
        self.at, self.both, self.cols, self.chunks = at, both, cols, chunks
        self.own_sem, self.zs, self.zr, self.fs, self.ys, self.yr, self.cs, self.cr = sems
        self.size = 2 * COEFS // chunks

    def block(self, ch, z, y=None, c=None):
        at = self.at
        return self.cols.at[
            pl.ds(ch * self.size, self.size), z, at.y if y is None else y, at.c if c is None else c
        ]

    def mine(self, ch, x):
        return self.both.at[x, pl.ds(ch * self.size, self.size)]

    def own(self, ch):
        return pltpu.make_async_copy(self.mine(ch, self.at.half), self.block(ch, self.at.z), self.own_sem.at[ch])

    def to_pair(self, ch):
        at = self.at
        return rcopy(
            self.mine(ch, at.half), self.block(ch, at.z), self.zs.at[ch, 0], self.zr.at[ch, at.z], at.slab(z=at.pair)
        )

    def to_gate(self, ch):
        at = self.at
        return rcopy(
            self.mine(ch, 1 - at.half), self.block(ch, at.z), self.zs.at[ch, 1], self.zr.at[ch, at.z], at.slab(z=at.near)
        )

    def onward(self, ch, z, i):
        at = self.at
        return rcopy(self.block(ch, z), self.block(ch, z), self.fs.at[ch, i], self.zr.at[ch, z], at.slab(z=at.pair))

    def z_arrival(self, ch, z):
        return rcopy(self.block(ch, z), self.block(ch, z), self.fs.at[ch, 0], self.zr.at[ch, z], self.at.slab(z=self.at.pair))

    def across(self, ch, z, src=None):
        at = self.at
        src = self.block(ch, z) if src is None else src
        return rcopy(src, self.block(ch, z), self.ys.at[ch, z], self.yr.at[ch, z], at.slab(y=1 - at.y))

    def y_arrival(self, ch, z):
        at = self.at
        dst = self.block(ch, z, y=1 - at.y)
        return rcopy(dst, dst, self.ys.at[ch, z], self.yr.at[ch, z], at.slab(y=1 - at.y))

    def core(self, ch, c=None):
        at = self.at
        dst = self.cols.at[pl.ds(ch * self.size, self.size), :, :, at.c if c is None else c]
        return rcopy(dst, dst, self.cs.at[ch], self.cr.at[ch], at.slab(c=1 - at.c))

    def start(self, ch):
        self.own(ch).start()
        self.to_gate(ch).start()
        self.to_pair(ch).start()
        self.across(ch, self.at.z, self.mine(ch, self.at.half)).start()

    def on_z(self, ch):
        at = self.at
        self.z_arrival(ch, at.pair).wait_recv()
        self.across(ch, at.pair).start()
        for i, z in enumerate((at.near, at.far)):
            self.z_arrival(ch, z).wait_recv()

            @pl.when(at.gate)
            def _():
                self.onward(ch, z, i).start()

            self.across(ch, z).start()

    def on_y(self, ch):
        self.own(ch).wait()
        for z in range(4):
            self.y_arrival(ch, z).wait_recv()
        self.core(ch).start()

    def on_core(self, ch):
        self.core(ch, 1 - self.at.c).wait_recv()

    def finish(self, ch):
        at = self.at
        self.to_gate(ch).wait_send()
        self.to_pair(ch).wait_send()
        self.across(ch, at.z, self.mine(ch, at.half)).wait_send()
        for z in (at.pair, at.near, at.far):
            self.across(ch, z).wait_send()

        @pl.when(at.gate)
        def _():
            for i, z in enumerate((at.near, at.far)):
                self.onward(ch, z, i).wait_send()

        self.core(ch).wait_send()


def gather_sems(chunks):
    dma = pltpu.SemaphoreType.DMA
    return [
        dma((chunks,)),
        dma((chunks, 2)),
        dma((chunks, 4)),
        dma((chunks, 2)),
        dma((chunks, 4)),
        dma((chunks, 4)),
        dma((chunks,)),
        dma((chunks,)),
    ]


class Scatter:
    def __init__(self, at, part, step, out, bufs, sems, chunks):
        self.at, self.part, self.step, self.out = at, part, step, out
        self.from_core, self.from_y, self.from_z, self.from_far = bufs
        self.cs, self.cr, self.ys, self.yr, self.zs, self.zr, self.fs, self.fr = sems
        self.size = COEFS // chunks

    def ks(self, ch):
        return pl.ds(ch * self.size, self.size)

    def core(self, ch):
        at = self.at
        return rcopy(
            self.part.at[self.ks(ch), :, :, 1 - at.c],
            self.from_core.at[self.ks(ch)],
            self.cs.at[ch],
            self.cr.at[ch],
            at.slab(c=1 - at.c),
        )

    def across(self, ch):
        at = self.at
        return rcopy(
            self.from_core.at[self.ks(ch), :, 1 - at.y],
            self.from_y.at[self.ks(ch)],
            self.ys.at[ch],
            self.yr.at[ch],
            at.slab(y=1 - at.y),
        )

    def inward(self, ch):
        at = self.at
        rows = pl.ds(1 - at.half, 3)
        return rcopy(
            self.from_y.at[self.ks(ch), rows],
            self.from_z.at[self.ks(ch), rows],
            self.zs.at[ch],
            self.zr.at[ch],
            at.slab(z=at.pair),
        )

    def outward(self, ch, z):
        at = self.at
        return rcopy(
            self.from_y.at[self.ks(ch), z],
            self.from_z.at[self.ks(ch), z],
            self.zs.at[ch],
            self.zr.at[ch],
            at.slab(z=at.pair),
        )

    def home(self, ch, z, i):
        at = self.at
        return rcopy(
            self.from_z.at[self.ks(ch), z], self.from_far.at[self.ks(ch)], self.fs.at[ch, i], self.fr.at[ch], at.slab(z=z)
        )

    def start(self, ch):
        self.core(ch).start()

    def on_core(self, ch):
        at, ks = self.at, self.ks(ch)
        self.core(ch).wait_recv()
        self.from_core[ks] += self.part[ks, :, :, at.c]
        self.across(ch).start()

    def on_y(self, ch):
        at, ks = self.at, self.ks(ch)
        self.across(ch).wait_recv()
        self.from_y[ks] += self.from_core[ks, :, at.y]

        @pl.when(at.gate)
        def _():
            self.outward(ch, at.pair).start()

        @pl.when(jnp.logical_not(at.gate))
        def _():
            self.inward(ch).start()

    def on_z(self, ch):
        at, ks = self.at, self.ks(ch)

        @pl.when(at.gate)
        def _():
            self.inward(ch).wait_recv()
            for i, z in enumerate((at.near, at.far)):
                self.from_z[ks, z] += self.from_y[ks, z]
                self.home(ch, z, i).start()

        @pl.when(jnp.logical_not(at.gate))
        def _():
            self.outward(ch, at.z).wait_recv()

        self.out[at.half, ks] = self.from_y[ks, at.z] + self.from_z[ks, at.z] + ALPHA * self.step[at.half, ks]

    def on_far(self, ch):
        at, ks = self.at, self.ks(ch)
        self.home(ch, at.near, 0).wait_recv()
        self.out[1 - at.half, ks] = self.from_far[ks] + ALPHA * self.step[1 - at.half, ks]

    def finish(self, ch):
        at = self.at
        self.core(ch).wait_send()
        self.across(ch).wait_send()

        @pl.when(at.gate)
        def _():
            self.outward(ch, at.pair).wait_send()
            for i, z in enumerate((at.near, at.far)):
                self.home(ch, z, i).wait_send()

        @pl.when(jnp.logical_not(at.gate))
        def _():
            self.inward(ch).wait_send()


def scatter_scratch():
    return [
        pltpu.VMEM((COEFS, 4, 2, 8, 2 * NY), F32),
        pltpu.VMEM((COEFS, 4, 8, 2 * NY), F32),
        pltpu.VMEM((COEFS, 4, 8, 2 * NY), F32),
        pltpu.VMEM((COEFS, 8, 2 * NY), F32),
    ]


def scatter_sems(chunks):
    dma = pltpu.SemaphoreType.DMA
    return [dma((chunks,))] * 6 + [dma((chunks, 2)), dma((chunks,))]


PAIR_ROWS = 80
FRAME_ROWS = 32


def gram_operands(temporal_basis, sample_mask):
    first = np.array([p[0] for p in PAIRS])
    second = np.array([p[1] for p in PAIRS])
    pick_first = jnp.asarray(np.eye(COEFS, dtype=np.float32)[first])
    pick_second = jnp.asarray(np.eye(COEFS, dtype=np.float32)[second])
    left = jnp.einsum("qk,tk->qt", pick_first, temporal_basis, precision=lax.Precision.HIGHEST)
    right = jnp.einsum("qk,tk->qt", pick_second, temporal_basis, precision=lax.Precision.HIGHEST)
    outer = jnp.pad(left * right, ((0, PAIR_ROWS - len(PAIRS)), (0, FRAME_ROWS - FRAMES)))
    mask = sample_mask.T.reshape(HY, 2, NZ).transpose(1, 0, 2).reshape(NY, NZ)
    return outer, mask


def gram_tiles(first, count, outer, mask, gram):
    high, low = split(outer[...])
    least = (outer[...] - high.astype(F32) - low.astype(F32)).astype(BF16)
    table = jnp.concatenate([high, low, least], axis=1)
    frame = lax.broadcasted_iota(jnp.int32, (FRAME_ROWS, NZ), 0)

    @pl.loop(first, first + count)
    def _(tile):
        words = mask[pl.ds(pl.multiple_of(tile * 8, 8), 8), :]
        for r in range(0, 8, 2):
            bits = []
            for j in range(2):
                word = jnp.broadcast_to(words[r + j : r + j + 1], (FRAME_ROWS, NZ))
                bits.append(jnp.bitwise_and(jnp.right_shift(word, frame), 1).astype(F32).astype(BF16))
            once = jnp.concatenate(bits, axis=1)
            out = jnp.dot(table, jnp.concatenate([once] * 3, axis=0), preferred_element_type=F32)
            for j in range(2):
                gram[pl.ds(tile * 8 + r + j, PAIR_ROWS, stride=NY), :] = out[:, j * NZ : (j + 1) * NZ]


def fused_kernel(
    items, both, coil, step, home, outer, mask, yl, yr, zt, weights, grad_out, spec_out,
    cols, colt, img, spec, grad, back, part, gram, *rest
):
    chunks = COEFS // 2
    at = Place()
    greet(at)
    g = Gather(at, both, cols, rest[:8], chunks)
    s = Scatter(at, part, home, grad_out, rest[8:12], rest[12:], chunks)
    tiles = NY // 8 // 3
    for ch in range(3):
        g.start(ch)
    gram_tiles(0, tiles, outer, mask, gram)
    g.on_z(0)
    g.start(3)
    gram_tiles(tiles, tiles, outer, mask, gram)
    g.on_z(1)
    g.start(4)
    g.on_y(0)
    gram_tiles(2 * tiles, tiles, outer, mask, gram)
    g.on_z(2)
    g.start(5)
    g.on_y(1)
    coil_images(items, coil, step, weights, yr, zt, img)
    back[...] = jnp.zeros_like(back)
    for ch in range(chunks):
        if ch + 3 < chunks:
            g.on_z(ch + 3)
        if ch + 2 < chunks:
            g.on_y(ch + 2)
        g.on_core(ch)
        transposed_in(cols, colt, 4 * ch, 4)
        forward_pass(items, ch, 1, colt, img, spec, yl, zt)
    for ch in range(chunks):
        g.finish(ch)
    mix_pass(items, gram, spec)

    def stages(ch):
        for late, stage in ((1, s.on_core), (2, s.on_y), (3, s.on_z)):
            if 0 <= ch - late < chunks:
                stage(ch - late)

    for ch in range(chunks):
        inverse_pass(items, ch, 1, colt, img, spec, grad, back, yl, zt)
        for k in (2 * ch, 2 * ch + 1):
            part[k] = grad[k].reshape(2 * NY, NZ).T.reshape(4, 2, 2, 8, 2 * NY)
        s.start(ch)
        stages(ch)
    for i in range(items):
        coil_gradients(i, 1, back, step, weights, yr, zt, spec_out)
        stages(chunks + i)
    for ch in range(chunks + items, chunks + 3):
        stages(ch)
    for ch in range(chunks):
        s.on_far(ch)
    for ch in range(chunks):
        s.finish(ch)


def fused(both, coil, step, home, outer, mask):
    items = coil.shape[0]
    chunks = COEFS // 2
    tables = make_tables()
    vmem = pl.BlockSpec(memory_space=pltpu.VMEM)
    return pl.pallas_call(
        functools.partial(fused_kernel, items),
        out_shape=(jax.ShapeDtypeStruct(home.shape, F32), jax.ShapeDtypeStruct(coil.shape, F32)),
        in_specs=[vmem] * 10,
        out_specs=(vmem, vmem),
        scratch_shapes=[
            pltpu.VMEM((2 * COEFS, 4, 2, 2, 8, 2 * NY), F32),
            pltpu.VMEM((2 * COEFS, 2, NY, NZ), F32),
            pltpu.VMEM((items, 2, 2, NY, NZ), F32),
            pltpu.VMEM((items, COEFS, 2, NY, NZ), F32),
            pltpu.VMEM((COEFS, 2, NY, NZ), F32),
            pltpu.VMEM((items, 2, NY, NZ), F32),
            pltpu.VMEM((COEFS, 4, 2, 2, 8, 2 * NY), F32),
            pltpu.VMEM((PAIR_ROWS * NY, NZ), F32),
        ]
        + gather_sems(chunks)
        + scatter_scratch()
        + scatter_sems(chunks),
        compiler_params=pltpu.CompilerParams(collective_id=0, has_side_effects=True, vmem_limit_bytes=56 * 2**20),
        cost_estimate=pl.CostEstimate(flops=16 * 10**9, bytes_accessed=20 * 2**20, transcendentals=0),
    )(both, coil, step, home, outer, mask, *[jnp.asarray(t) for t in tables])


def shards(image_coef, step_coef, coil_spec, step_spec, temporal_basis, sample_mask):
    devices = lax.axis_size("slab")
    width_x, _, rows_z, _ = image_coef.shape
    both = jnp.stack([image_coef, step_coef], axis=2).reshape(width_x, 2 * COEFS, rows_z, 2 * NY)
    if devices == 16 and width_x == 2 and rows_z == 8:
        outer, mask = gram_operands(temporal_basis, sample_mask)
        return fused(both, coil_spec, step_spec, step_coef, outer, mask)
    else:
        cols = gather_plain(both, devices)
        gram = gram_planes(temporal_basis, sample_mask).reshape(len(PAIRS) * NY, NZ)
        part, grad_spec = compute(cols, coil_spec, step_spec, gram)
        grad_coef = scatter_plain(part, width_x, devices) + ALPHA * step_coef
    return grad_coef, grad_spec


def solution(mesh):
    in_specs = (
        P("scan", None, "slab", None),
        P("scan", None, "slab", None),
        P(("scan", "slab"), None, None),
        P(("scan", "slab"), None, None),
        P(),
        P("scan", None),
    )
    out_specs = (P("scan", None, "slab", None), P(("scan", "slab"), None, None))
    return jax.shard_map(shards, mesh=mesh, in_specs=in_specs, out_specs=out_specs, check_vma=False)
```

```python
import functools
import math

import jax
import jax.numpy as jnp
import ml_dtypes
import numpy as np
from jax import lax
from jax.experimental import pallas as pl
from jax.experimental.pallas import tpu as pltpu
from jax.sharding import PartitionSpec as P

NY = 192
NZ = 128
HY = NY // 2
COEFS = 12
FRAMES = 30
ALPHA = 0.5
SOBOLEV = 32.0
PAIRS = [(a, b) for a in range(COEFS) for b in range(a, COEFS)]
PAIR_AT = {p: i for i, p in enumerate(PAIRS)}
F32 = jnp.float32
BF16 = jnp.bfloat16


def complex_table(rows, cols, length, sign):
    idx = (np.asarray(rows)[:, None] * np.asarray(cols)[None, :]) % length
    angles = 2.0 * math.pi * idx / length
    scale = 1.0 / math.sqrt(length)
    return np.cos(angles) * scale, np.sin(angles) * (scale * sign)


def split_np(table):
    high = table.astype(np.float32).astype(ml_dtypes.bfloat16)
    low = (table - high.astype(np.float64)).astype(np.float32).astype(ml_dtypes.bfloat16)
    return high, low


def right_table(length, sign):
    c, s = complex_table(range(length), range(length), length, sign)
    high, low = split_np(np.block([[c, s], [-s, c]]))
    return np.concatenate([high, low, high], axis=0)


def left_table(rows, cols, length, sign):
    c, s = complex_table(rows, cols, length, sign)
    high, low = split_np(np.block([[c, -s], [s, c]]))
    return np.concatenate([high, high, low], axis=1)


EVEN = np.arange(0, NY, 2)
ODD = np.arange(1, NY, 2)
NEAR = np.arange(HY)


def make_tables():
    y_left = np.stack(
        [
            left_table(EVEN, NEAR, NY, -1.0),
            left_table(ODD, NEAR, NY, -1.0),
            left_table(NEAR, EVEN, NY, 1.0),
            left_table(NEAR, ODD, NY, 1.0),
        ]
    )
    y_right = np.stack([right_table(NY, -1.0), right_table(NY, 1.0)])
    z_right = np.stack([right_table(NZ, -1.0), right_table(NZ, 1.0)])
    fz = ((np.arange(NZ) + NZ // 2) % NZ - NZ // 2) / NZ
    fy = ((np.arange(NY) + NY // 2) % NY - NY // 2) / NY
    plane = 1.0 / (1.0 + SOBOLEV * (fz[:, None] ** 2 + fy[None, :] ** 2)) ** 2
    weights = np.concatenate([plane, plane], axis=1).astype(np.float32)
    return y_left, y_right, z_right, weights


def split(x):
    high = x.astype(BF16)
    low = (x - high.astype(F32)).astype(BF16)
    return high, low


def times_right(x, table):
    high, low = split(x)
    return jnp.dot(jnp.concatenate([high, high, low], axis=1), table, preferred_element_type=F32)


def times_left(table, x):
    high, low = split(x)
    return jnp.dot(table, jnp.concatenate([high, low, high], axis=0), preferred_element_type=F32)


def z_stage(re, im, table):
    out = times_right(jnp.concatenate([re, im], axis=1), table)
    return out[:, :NZ], out[:, NZ:]


def forward(planes, yl, zt):
    ups, downs = [], []
    for re, im in planes:
        ups.append(jnp.concatenate([re[:HY] + re[HY:], im[:HY] + im[HY:]], axis=0))
        downs.append(jnp.concatenate([re[:HY] - re[HY:], im[:HY] - im[HY:]], axis=0))
    even = times_left(yl[0], jnp.concatenate(ups, axis=1))
    odd = times_left(yl[1], jnp.concatenate(downs, axis=1))
    outs = []
    for i in range(2):
        at = slice(i * NZ, (i + 1) * NZ)
        re = jnp.concatenate([even[:HY, at], odd[:HY, at]], axis=0)
        im = jnp.concatenate([even[HY:, at], odd[HY:, at]], axis=0)
        outs.append(z_stage(re, im, zt[0]))
    return outs


def inverse(planes, yl, zt):
    evens, odds = [], []
    for re, im in planes:
        re, im = z_stage(re, im, zt[1])
        evens.append(jnp.concatenate([re[:HY], im[:HY]], axis=0))
        odds.append(jnp.concatenate([re[HY:], im[HY:]], axis=0))
    even = times_left(yl[2], jnp.concatenate(evens, axis=1))
    odd = times_left(yl[3], jnp.concatenate(odds, axis=1))
    near, far = even + odd, even - odd
    outs = []
    for i in range(2):
        at = slice(i * NZ, (i + 1) * NZ)
        re = jnp.concatenate([near[:HY, at], far[:HY, at]], axis=0)
        im = jnp.concatenate([near[HY:, at], far[HY:, at]], axis=0)
        outs.append((re, im))
    return outs


def coil_images(items, coil_ref, step_ref, weights, yr, zt, img):
    @pl.loop(0, items)
    def _(i):
        for which, ref in enumerate((coil_ref, step_ref)):
            rows = times_right(ref[i] * weights[...], yr[1])
            t = rows.T
            re, im = z_stage(t[:NY], t[NY:], zt[1])
            img[i, which, 0] = re
            img[i, which, 1] = im


def transposed_in(cols, colt, first, count):
    @pl.loop(first, first + count, unroll=2)
    def _(p):
        colt[p] = cols[p].reshape(NZ, 2 * NY).T.reshape(2, NY, NZ)


def forward_pass(items, first_pair, pair_count, colt, img, spec, yl, zt):
    @pl.loop(first_pair * items, (first_pair + pair_count) * items, unroll=items if pair_count == 1 else None)
    def _(step):
        pair, i = step // items, step % items
        planes = []
        for j in range(2):
            k = 2 * pair + j
            cr, ci = colt[2 * k, 0], colt[2 * k, 1]
            sr, si = colt[2 * k + 1, 0], colt[2 * k + 1, 1]
            ar, ai = img[i, 0, 0], img[i, 0, 1]
            dr, di = img[i, 1, 0], img[i, 1, 1]
            planes.append((ar * sr - ai * si + dr * cr - di * ci, ar * si + ai * sr + dr * ci + di * cr))
        for j, (re, im) in enumerate(forward(planes, yl, zt)):
            spec[i, 2 * pair + j, 0] = re
            spec[i, 2 * pair + j, 1] = im


def mix_pass(items, gram, spec):
    @pl.loop(0, NY // 8)
    def _(tile):
        rows = pl.ds(pl.multiple_of(tile * 8, 8), 8)
        for i in range(items):
            re = [spec[i, k, 0, rows, :] for k in range(COEFS)]
            im = [spec[i, k, 1, rows, :] for k in range(COEFS)]
            for k in range(COEFS):
                acc_re = acc_im = None
                for m in range(COEFS):
                    first = PAIR_AT[(min(k, m), max(k, m))] * NY + tile * 8
                    g = gram[pl.ds(pl.multiple_of(first, 8), 8), :]
                    acc_re = g * re[m] if acc_re is None else acc_re + g * re[m]
                    acc_im = g * im[m] if acc_im is None else acc_im + g * im[m]
                spec[i, k, 0, rows, :] = acc_re
                spec[i, k, 1, rows, :] = acc_im


def inverse_pass(items, first_pair, pair_count, colt, img, spec, grad, back, yl, zt):
    @pl.loop(first_pair * items, (first_pair + pair_count) * items, unroll=items if pair_count == 1 else None)
    def _(step):
        pair, i = step // items, step % items
        outs = inverse([(spec[i, 2 * pair + j, 0], spec[i, 2 * pair + j, 1]) for j in range(2)], yl, zt)
        ar, ai = img[i, 0, 0], img[i, 0, 1]
        back_re, back_im = back[i, 0], back[i, 1]
        for j, (re, im) in enumerate(outs):
            k = 2 * pair + j
            cr, ci = colt[2 * k, 0], colt[2 * k, 1]
            back_re += cr * re + ci * im
            back_im += cr * im - ci * re
            grad_re = ar * re + ai * im
            grad_im = ar * im - ai * re

            @pl.when(i == 0)
            def _():
                grad[k, 0] = grad_re
                grad[k, 1] = grad_im

            @pl.when(i > 0)
            def _():
                grad[k, 0] += grad_re
                grad[k, 1] += grad_im

        back[i, 0] = back_re
        back[i, 1] = back_im


def coil_gradients(first, count, back, step_ref, weights, yr, zt, out):
    @pl.loop(first, first + count)
    def _(i):
        re, im = z_stage(back[i, 0], back[i, 1], zt[0])
        rows = jnp.concatenate([re, im], axis=0).T
        out[i] = times_right(rows, yr[0]) * weights[...] + ALPHA * step_ref[i]


def compute_kernel(items, cols, coil, step, gram, yl, yr, zt, weights, part, spec_out, colt, img, spec, grad, back):
    coil_images(items, coil, step, weights, yr, zt, img)
    transposed_in(cols, colt, 0, 2 * COEFS)
    back[...] = jnp.zeros_like(back)
    forward_pass(items, 0, COEFS // 2, colt, img, spec, yl, zt)
    mix_pass(items, gram, spec)
    inverse_pass(items, 0, COEFS // 2, colt, img, spec, grad, back, yl, zt)

    @pl.loop(0, COEFS)
    def _(k):
        part[k] = grad[k].reshape(2 * NY, NZ).T

    coil_gradients(0, items, back, step, weights, yr, zt, spec_out)


def compute(cols, coil, step, gram):
    items = coil.shape[0]
    tables = make_tables()
    vmem = pl.BlockSpec(memory_space=pltpu.VMEM)
    return pl.pallas_call(
        functools.partial(compute_kernel, items),
        out_shape=(
            jax.ShapeDtypeStruct((COEFS, NZ, 2 * NY), F32),
            jax.ShapeDtypeStruct(coil.shape, F32),
        ),
        in_specs=[vmem] * 8,
        out_specs=(vmem, vmem),
        scratch_shapes=[
            pltpu.VMEM((2 * COEFS, 2, NY, NZ), F32),
            pltpu.VMEM((items, 2, 2, NY, NZ), F32),
            pltpu.VMEM((items, COEFS, 2, NY, NZ), F32),
            pltpu.VMEM((COEFS, 2, NY, NZ), F32),
            pltpu.VMEM((items, 2, NY, NZ), F32),
        ],
        compiler_params=pltpu.CompilerParams(vmem_limit_bytes=56 * 2**20),
        cost_estimate=pl.CostEstimate(flops=16 * 10**9, bytes_accessed=20 * 2**20, transcendentals=0),
    )(cols, coil, step, gram, *[jnp.asarray(t) for t in tables])


def gram_planes(temporal_basis, sample_mask):
    first = np.array([p[0] for p in PAIRS])
    second = np.array([p[1] for p in PAIRS])
    outer = (temporal_basis[:, first] * temporal_basis[:, second]).T
    mask = sample_mask.T.reshape(HY, 2, NZ).transpose(1, 0, 2).reshape(NY, NZ)
    frames = jnp.arange(FRAMES, dtype=jnp.int32)
    bits = jnp.bitwise_and(jnp.right_shift(mask[None], frames[:, None, None]), 1).astype(F32)
    return jnp.einsum("qt,tyz->qyz", outer, bits, precision=lax.Precision.HIGHEST)


def gather_plain(both, devices):
    width_x = both.shape[0]
    groups = devices // width_x
    rep = jnp.broadcast_to(both[:, None], (width_x, groups) + both.shape[1:])
    rep = rep.reshape((devices * both.shape[1],) + both.shape[2:])
    return lax.all_to_all(rep, "slab", split_axis=0, concat_axis=1, tiled=True)


def scatter_plain(part, width_x, devices):
    homed = lax.all_to_all(part, "slab", split_axis=1, concat_axis=0, tiled=True)
    rows = part.shape[1] // devices
    return jnp.sum(homed.reshape(width_x, devices // width_x, COEFS, rows, 2 * NY), axis=1)


MESH = pl.DeviceIdType.MESH


class Place:
    def __init__(self):
        me = lax.axis_index("slab")
        self.z, self.y, self.c = me // 4, (me // 2) % 2, me % 2
        self.half = self.z // 2
        self.pair = 4 * self.half + 1 - self.z
        self.near = 2 - self.half
        self.far = 3 - 3 * self.half
        self.gate = self.z == 1 + self.half

    def slab(self, z=None, y=None, c=None):
        z = self.z if z is None else z
        y = self.y if y is None else y
        c = self.c if c is None else c
        return z * 4 + y * 2 + c


def rcopy(src, dst, send, recv, slab):
    return pltpu.make_async_remote_copy(
        src_ref=src, dst_ref=dst, send_sem=send, recv_sem=recv, device_id={"slab": slab}, device_id_type=MESH
    )


def greet(at):
    barrier = pltpu.get_barrier_semaphore()

    def hello(slab):
        pl.semaphore_signal(barrier, inc=1, device_id={"slab": slab}, device_id_type=MESH)

    hello(at.slab(z=at.pair))
    hello(at.slab(y=1 - at.y))
    hello(at.slab(c=1 - at.c))
    hello(at.slab(z=at.near))

    @pl.when(at.gate)
    def _():
        hello(at.slab(z=at.far))
        pl.semaphore_wait(barrier, 5)

    @pl.when(jnp.logical_not(at.gate))
    def _():
        pl.semaphore_wait(barrier, 4)


class Gather:
    def __init__(self, at, both, cols, sems, chunks):
        self.at, self.both, self.cols, self.chunks = at, both, cols, chunks
        self.own_sem, self.zs, self.zr, self.fs, self.ys, self.yr, self.cs, self.cr = sems
        self.size = 2 * COEFS // chunks

    def block(self, ch, z, y=None, c=None):
        at = self.at
        return self.cols.at[
            pl.ds(ch * self.size, self.size), z, at.y if y is None else y, at.c if c is None else c
        ]

    def mine(self, ch, x):
        return self.both.at[x, pl.ds(ch * self.size, self.size)]

    def own(self, ch):
        return pltpu.make_async_copy(self.mine(ch, self.at.half), self.block(ch, self.at.z), self.own_sem.at[ch])

    def to_pair(self, ch):
        at = self.at
        return rcopy(
            self.mine(ch, at.half), self.block(ch, at.z), self.zs.at[ch, 0], self.zr.at[ch, at.z], at.slab(z=at.pair)
        )

    def to_gate(self, ch):
        at = self.at
        return rcopy(
            self.mine(ch, 1 - at.half), self.block(ch, at.z), self.zs.at[ch, 1], self.zr.at[ch, at.z], at.slab(z=at.near)
        )

    def onward(self, ch, z, i):
        at = self.at
        return rcopy(self.block(ch, z), self.block(ch, z), self.fs.at[ch, i], self.zr.at[ch, z], at.slab(z=at.pair))

    def z_arrival(self, ch, z):
        return rcopy(self.block(ch, z), self.block(ch, z), self.fs.at[ch, 0], self.zr.at[ch, z], self.at.slab(z=self.at.pair))

    def across(self, ch, z, src=None):
        at = self.at
        src = self.block(ch, z) if src is None else src
        return rcopy(src, self.block(ch, z), self.ys.at[ch, z], self.yr.at[ch, z], at.slab(y=1 - at.y))

    def y_arrival(self, ch, z):
        at = self.at
        dst = self.block(ch, z, y=1 - at.y)
        return rcopy(dst, dst, self.ys.at[ch, z], self.yr.at[ch, z], at.slab(y=1 - at.y))

    def core(self, ch, c=None):
        at = self.at
        dst = self.cols.at[pl.ds(ch * self.size, self.size), :, :, at.c if c is None else c]
        return rcopy(dst, dst, self.cs.at[ch], self.cr.at[ch], at.slab(c=1 - at.c))

    def start(self, ch):
        self.own(ch).start()
        self.to_gate(ch).start()
        self.to_pair(ch).start()
        self.across(ch, self.at.z, self.mine(ch, self.at.half)).start()

    def on_z(self, ch):
        at = self.at
        self.z_arrival(ch, at.pair).wait_recv()
        self.across(ch, at.pair).start()
        for i, z in enumerate((at.near, at.far)):
            self.z_arrival(ch, z).wait_recv()

            @pl.when(at.gate)
            def _():
                self.onward(ch, z, i).start()

            self.across(ch, z).start()

    def on_y(self, ch):
        self.own(ch).wait()
        for z in range(4):
            self.y_arrival(ch, z).wait_recv()
        self.core(ch).start()

    def on_core(self, ch):
        self.core(ch, 1 - self.at.c).wait_recv()

    def finish(self, ch):
        at = self.at
        self.to_gate(ch).wait_send()
        self.to_pair(ch).wait_send()
        self.across(ch, at.z, self.mine(ch, at.half)).wait_send()
        for z in (at.pair, at.near, at.far):
            self.across(ch, z).wait_send()

        @pl.when(at.gate)
        def _():
            for i, z in enumerate((at.near, at.far)):
                self.onward(ch, z, i).wait_send()

        self.core(ch).wait_send()


def gather_sems(chunks):
    dma = pltpu.SemaphoreType.DMA
    return [
        dma((chunks,)),
        dma((chunks, 2)),
        dma((chunks, 4)),
        dma((chunks, 2)),
        dma((chunks, 4)),
        dma((chunks, 4)),
        dma((chunks,)),
        dma((chunks,)),
    ]


class Scatter:
    def __init__(self, at, part, step, out, bufs, sems, chunks):
        self.at, self.part, self.step, self.out = at, part, step, out
        self.from_core, self.from_y, self.from_z, self.from_far = bufs
        self.cs, self.cr, self.ys, self.yr, self.zs, self.zr, self.fs, self.fr = sems
        self.size = COEFS // chunks

    def ks(self, ch):
        return pl.ds(ch * self.size, self.size)

    def core(self, ch):
        at = self.at
        return rcopy(
            self.part.at[self.ks(ch), :, :, 1 - at.c],
            self.from_core.at[self.ks(ch)],
            self.cs.at[ch],
            self.cr.at[ch],
            at.slab(c=1 - at.c),
        )

    def across(self, ch):
        at = self.at
        return rcopy(
            self.from_core.at[self.ks(ch), :, 1 - at.y],
            self.from_y.at[self.ks(ch)],
            self.ys.at[ch],
            self.yr.at[ch],
            at.slab(y=1 - at.y),
        )

    def inward(self, ch):
        at = self.at
        rows = pl.ds(1 - at.half, 3)
        return rcopy(
            self.from_y.at[self.ks(ch), rows],
            self.from_z.at[self.ks(ch), rows],
            self.zs.at[ch],
            self.zr.at[ch],
            at.slab(z=at.pair),
        )

    def outward(self, ch, z):
        at = self.at
        return rcopy(
            self.from_y.at[self.ks(ch), z],
            self.from_z.at[self.ks(ch), z],
            self.zs.at[ch],
            self.zr.at[ch],
            at.slab(z=at.pair),
        )

    def home(self, ch, z, i):
        at = self.at
        return rcopy(
            self.from_z.at[self.ks(ch), z], self.from_far.at[self.ks(ch)], self.fs.at[ch, i], self.fr.at[ch], at.slab(z=z)
        )

    def start(self, ch):
        self.core(ch).start()

    def on_core(self, ch):
        at, ks = self.at, self.ks(ch)
        self.core(ch).wait_recv()
        self.from_core[ks] += self.part[ks, :, :, at.c]
        self.across(ch).start()

    def on_y(self, ch):
        at, ks = self.at, self.ks(ch)
        self.across(ch).wait_recv()
        self.from_y[ks] += self.from_core[ks, :, at.y]

        @pl.when(at.gate)
        def _():
            self.outward(ch, at.pair).start()

        @pl.when(jnp.logical_not(at.gate))
        def _():
            self.inward(ch).start()

    def on_z(self, ch):
        at, ks = self.at, self.ks(ch)

        @pl.when(at.gate)
        def _():
            self.inward(ch).wait_recv()
            for i, z in enumerate((at.near, at.far)):
                self.from_z[ks, z] += self.from_y[ks, z]
                self.home(ch, z, i).start()

        @pl.when(jnp.logical_not(at.gate))
        def _():
            self.outward(ch, at.z).wait_recv()

        self.out[at.half, ks] = self.from_y[ks, at.z] + self.from_z[ks, at.z] + ALPHA * self.step[at.half, ks]

    def on_far(self, ch):
        at, ks = self.at, self.ks(ch)
        self.home(ch, at.near, 0).wait_recv()
        self.out[1 - at.half, ks] = self.from_far[ks] + ALPHA * self.step[1 - at.half, ks]

    def finish(self, ch):
        at = self.at
        self.core(ch).wait_send()
        self.across(ch).wait_send()

        @pl.when(at.gate)
        def _():
            self.outward(ch, at.pair).wait_send()
            for i, z in enumerate((at.near, at.far)):
                self.home(ch, z, i).wait_send()

        @pl.when(jnp.logical_not(at.gate))
        def _():
            self.inward(ch).wait_send()


def scatter_scratch():
    return [
        pltpu.VMEM((COEFS, 4, 2, 8, 2 * NY), F32),
        pltpu.VMEM((COEFS, 4, 8, 2 * NY), F32),
        pltpu.VMEM((COEFS, 4, 8, 2 * NY), F32),
        pltpu.VMEM((COEFS, 8, 2 * NY), F32),
    ]


def scatter_sems(chunks):
    dma = pltpu.SemaphoreType.DMA
    return [dma((chunks,))] * 6 + [dma((chunks, 2)), dma((chunks,))]


PAIR_ROWS = 80
FRAME_ROWS = 32


def gram_operands(temporal_basis, sample_mask):
    first = np.array([p[0] for p in PAIRS])
    second = np.array([p[1] for p in PAIRS])
    picks = np.zeros((2 * PAIR_ROWS, COEFS), np.float32)
    picks[np.arange(len(PAIRS)), first] = 1.0
    picks[PAIR_ROWS + np.arange(len(PAIRS)), second] = 1.0
    basis = jnp.pad(temporal_basis, ((0, FRAME_ROWS - FRAMES), (0, 0)))
    mask = sample_mask.T.reshape(HY, 2, NZ).transpose(1, 0, 2).reshape(NY, NZ)
    return basis, jnp.asarray(picks), mask


def gram_tiles(first, count, outer, mask, gram):
    high, low = split(outer)
    least = (outer - high.astype(F32) - low.astype(F32)).astype(BF16)
    table = jnp.concatenate([high, low, least], axis=1)
    frame = lax.broadcasted_iota(jnp.int32, (FRAME_ROWS, NZ), 0)

    @pl.loop(first, first + count)
    def _(tile):
        words = mask[pl.ds(pl.multiple_of(tile * 8, 8), 8), :]
        for r in range(0, 8, 2):
            bits = []
            for j in range(2):
                word = jnp.broadcast_to(words[r + j : r + j + 1], (FRAME_ROWS, NZ))
                bits.append(jnp.bitwise_and(jnp.right_shift(word, frame), 1).astype(F32).astype(BF16))
            once = jnp.concatenate(bits, axis=1)
            out = jnp.dot(table, jnp.concatenate([once] * 3, axis=0), preferred_element_type=F32)
            for j in range(2):
                gram[pl.ds(tile * 8 + r + j, PAIR_ROWS, stride=NY), :] = out[:, j * NZ : (j + 1) * NZ]


def fused_kernel(
    items, both, coil, step, home, basis, picks, mask, yl, yr, zt, weights, grad_out, spec_out,
    cols, colt, img, spec, grad, back, part, gram, *rest
):
    chunks = COEFS // 2
    at = Place()
    greet(at)
    g = Gather(at, both, cols, rest[:8], chunks)
    s = Scatter(at, part, home, grad_out, rest[8:12], rest[12:], chunks)
    tiles = NY // 8 // 3
    for ch in range(3):
        g.start(ch)
    picked = lax.dot_general(
        picks[...], basis[...], (((1,), (1,)), ((), ())), precision=lax.Precision.HIGHEST, preferred_element_type=F32
    )
    outer = picked[:PAIR_ROWS] * picked[PAIR_ROWS:]
    gram_tiles(0, tiles, outer, mask, gram)
    g.on_z(0)
    g.start(3)
    gram_tiles(tiles, tiles, outer, mask, gram)
    g.on_z(1)
    g.start(4)
    g.on_y(0)
    gram_tiles(2 * tiles, tiles, outer, mask, gram)
    g.on_z(2)
    g.start(5)
    g.on_y(1)
    coil_images(items, coil, step, weights, yr, zt, img)
    back[...] = jnp.zeros_like(back)
    for ch in range(chunks):
        if ch + 3 < chunks:
            g.on_z(ch + 3)
        if ch + 2 < chunks:
            g.on_y(ch + 2)
        g.on_core(ch)
        transposed_in(cols, colt, 4 * ch, 4)
        forward_pass(items, ch, 1, colt, img, spec, yl, zt)
    for ch in range(chunks):
        g.finish(ch)
    mix_pass(items, gram, spec)

    def stages(ch):
        for late, stage in ((1, s.on_core), (2, s.on_y), (3, s.on_z)):
            if 0 <= ch - late < chunks:
                stage(ch - late)

    for ch in range(chunks):
        inverse_pass(items, ch, 1, colt, img, spec, grad, back, yl, zt)
        for k in (2 * ch, 2 * ch + 1):
            part[k] = grad[k].reshape(2 * NY, NZ).T.reshape(4, 2, 2, 8, 2 * NY)
        s.start(ch)
        stages(ch)
    for i in range(items):
        coil_gradients(i, 1, back, step, weights, yr, zt, spec_out)
        stages(chunks + i)
    for ch in range(chunks + items, chunks + 3):
        stages(ch)
    for ch in range(chunks):
        s.on_far(ch)
    for ch in range(chunks):
        s.finish(ch)


def fused(both, coil, step, home, basis, picks, mask):
    items = coil.shape[0]
    chunks = COEFS // 2
    tables = make_tables()
    vmem = pl.BlockSpec(memory_space=pltpu.VMEM)
    return pl.pallas_call(
        functools.partial(fused_kernel, items),
        out_shape=(jax.ShapeDtypeStruct(home.shape, F32), jax.ShapeDtypeStruct(coil.shape, F32)),
        in_specs=[vmem] * 11,
        out_specs=(vmem, vmem),
        scratch_shapes=[
            pltpu.VMEM((2 * COEFS, 4, 2, 2, 8, 2 * NY), F32),
            pltpu.VMEM((2 * COEFS, 2, NY, NZ), F32),
            pltpu.VMEM((items, 2, 2, NY, NZ), F32),
            pltpu.VMEM((items, COEFS, 2, NY, NZ), F32),
            pltpu.VMEM((COEFS, 2, NY, NZ), F32),
            pltpu.VMEM((items, 2, NY, NZ), F32),
            pltpu.VMEM((COEFS, 4, 2, 2, 8, 2 * NY), F32),
            pltpu.VMEM((PAIR_ROWS * NY, NZ), F32),
        ]
        + gather_sems(chunks)
        + scatter_scratch()
        + scatter_sems(chunks),
        compiler_params=pltpu.CompilerParams(collective_id=0, has_side_effects=True, vmem_limit_bytes=56 * 2**20),
        cost_estimate=pl.CostEstimate(flops=16 * 10**9, bytes_accessed=20 * 2**20, transcendentals=0),
    )(both, coil, step, home, basis, picks, mask, *[jnp.asarray(t) for t in tables])


def shards(image_coef, step_coef, coil_spec, step_spec, temporal_basis, sample_mask):
    devices = lax.axis_size("slab")
    width_x, _, rows_z, _ = image_coef.shape
    both = jnp.stack([image_coef, step_coef], axis=2).reshape(width_x, 2 * COEFS, rows_z, 2 * NY)
    if devices == 16 and width_x == 2 and rows_z == 8:
        basis, picks, mask = gram_operands(temporal_basis, sample_mask)
        return fused(both, coil_spec, step_spec, step_coef, basis, picks, mask)
    else:
        cols = gather_plain(both, devices)
        gram = gram_planes(temporal_basis, sample_mask).reshape(len(PAIRS) * NY, NZ)
        part, grad_spec = compute(cols, coil_spec, step_spec, gram)
        grad_coef = scatter_plain(part, width_x, devices) + ALPHA * step_coef
    return grad_coef, grad_spec


def solution(mesh):
    in_specs = (
        P("scan", None, "slab", None),
        P("scan", None, "slab", None),
        P(("scan", "slab"), None, None),
        P(("scan", "slab"), None, None),
        P(),
        P("scan", None),
    )
    out_specs = (P("scan", None, "slab", None), P(("scan", "slab"), None, None))
    return jax.shard_map(shards, mesh=mesh, in_specs=in_specs, out_specs=out_specs, check_vma=False)
```
